128 devices in a mesh: tm: 2 (over core), lon: 32 (over z, x, y_lo), cls: 2 (over y_hi).
Axes of the slice: x: 4, y: 4 (y_hi: 2, y_lo: 2; y = y_hi * 2 + y_lo), z: 4, core: 2. Of those that a mesh axis runs over, the one named last changes fastest.
Arguments:
- velocity: bfloat16 [32, 1024, 32, 256], P('tm', 'lon'), may hold values from -6 to 6
- thickness: bfloat16 [32, 1024, 32, 256], P('tm', 'lon'), may hold values from 0.25 to 4
- class_index: int32 [32, 1024, 32, 256], P('tm', 'lon'), may hold values from 0 to 238
- layer_weight: int32 [32, 1024, 32, 256], P('tm', 'lon'), may hold values from 0 to 64
- zonal_width: float32 [256], replicated, may hold values from 0.01 to 0.1
Outputs:
- psi_snap: float32 [32, 240, 256], P('tm', 'cls')
- psi_mean: float32 [240, 256], P('cls', ('tm', 'lon'))
- psi_var: float32 [240, 256], P('cls', ('tm', 'lon'))
The draws below stay inside these ranges and needn't reach their ends.
All inputs are finite; a program needn't handle non-finite values.
Results may differ from the reference program's by a relative error of at most 0.0003.
Values sent between devices are 32-bit elements; how exact they have to be, the bound alone decides.
A program may use at most 128 MiB of HBM per device.

```python
import math
import jax
import jax.numpy as jnp
from jax import lax

C = 240
ROWS = 256
LEVELS = 32
SNAPS = 32
LONS = 1024


def touch_ends(entries, stream_key, least, largest):
    longest = entries.shape.index(max(entries.shape))
    spots = []
    for shift in (0, 1):
        where = [jax.random.randint(jax.random.fold_in(stream_key, axis), (), 0, length) for axis, length in enumerate(entries.shape)]
        where[longest] = (where[longest] + shift) % entries.shape[longest]
        spots.append(tuple(where))
    return entries.at[spots[0]].set(least).at[spots[1]].set(largest)


def shard_levels(rng, extent, shards, least, high):
    def one(dim, parts):
        heights = jax.random.uniform(jax.random.fold_in(jax.random.fold_in(rng, 6), dim), (parts,), jnp.float32, least / len(shards), high / len(shards))
        return jnp.repeat(jnp.exp(heights), extent[dim] // parts).reshape((-1,) + (1,) * (len(extent) - dim - 1))

    level = one(*shards[0])
    for cut in shards[1:]:
        level = level * one(*cut)
    return level


def normal_values(rng, shape, deviation, bound, split=(), held_as=jnp.bfloat16):
    drawn = jax.random.normal(rng, shape, jnp.float32) * deviation
    if len(split) > 0:
        drawn = shard_levels(rng, shape, split, -0.22, 0.18) * drawn
    return jnp.clip(drawn, min=-bound, max=bound).astype(held_as)


def setup_inputs(seed: int = 0) -> dict:
    splits = jax.random.split(jax.random.key(seed), 6)
    velocity = normal_values(splits[0], (SNAPS, LONS, LEVELS, ROWS), 1.0, 6.0, ((0, 2), (1, 32)))
    thickness = jnp.clip(jnp.exp(math.log(4.0) - 2.7725887 * jax.random.uniform(splits[1], (SNAPS, LONS, LEVELS, ROWS), jnp.float32) ** shard_levels(splits[1], (SNAPS, LONS, LEVELS, ROWS), ((0, 2), (1, 32)), -0.2, 0.2)), 0.25, 4.0).astype(jnp.bfloat16)
    class_index = touch_ends(jax.random.randint(splits[2], (SNAPS, LONS, LEVELS, ROWS), 0, C - 1), jax.random.fold_in(splits[2], 1), 0, (C - 1) - 1).astype(jnp.int32)
    layer_weight = touch_ends(jax.random.randint(splits[3], (SNAPS, LONS, LEVELS, ROWS), 0, 65), jax.random.fold_in(splits[3], 1), 0, 64).astype(jnp.int32)
    zonal_width = jnp.clip(jnp.exp(jax.random.uniform(splits[4], (ROWS,), jnp.float32, math.log(0.01), math.log(0.1))), 0.01, 0.1)
    return dict(velocity=velocity, thickness=thickness, class_index=class_index, layer_weight=layer_weight, zonal_width=zonal_width)


def reference(velocity, thickness, class_index, layer_weight, zonal_width):
    def one_snapshot(items):
        speed, layer, lighter, share = items
        transport = speed.astype(jnp.float32) * layer.astype(jnp.float32) * zonal_width
        weight = share.astype(jnp.float32)
        first = transport * (weight / 64.0)
        second = transport * ((64.0 - weight) / 64.0)
        row_ids = lax.broadcasted_iota(jnp.int32, lighter.shape, 2)
        seg_first = lighter * ROWS + row_ids
        seg_second = (lighter + 1) * ROWS + row_ids
        segs = jnp.concatenate([seg_first.reshape(-1), seg_second.reshape(-1)])
        values = jnp.concatenate([first.reshape(-1), second.reshape(-1)])
        return jax.ops.segment_sum(values, segs, num_segments=C * ROWS).reshape(C, ROWS)

    binned = lax.map(one_snapshot, (velocity, thickness, class_index, layer_weight))
    psi_snap = jnp.cumsum(binned, axis=1)
    psi_mean = jnp.sum(psi_snap, axis=0) / SNAPS
    psi_var = jnp.sum(psi_snap * psi_snap, axis=0) / SNAPS - psi_mean * psi_mean
    return psi_snap, psi_mean, psi_var
```

```python
import functools
import jax
import jax.numpy as jnp
from jax import lax
from jax.experimental import pallas as pl
from jax.experimental.pallas import tpu as pltpu
from jax.sharding import PartitionSpec as P

C = 240
GROUPS = 8
NT = (((1,), (1,)), ((), ()))
MESH = pl.DeviceIdType.MESH
F32, BF16 = jnp.float32, jnp.bfloat16


def prepare(raw, turned, chunk):
    lons = pl.ds(chunk * 8, 8)
    cells = pl.ds(pl.multiple_of(chunk * 256, 256), 256)
    speed, layer, lighter, share = (ref[lons].reshape(256, 256) for ref in raw)
    v_t, h_t, hi_t, lo_t, q_t, e_t = turned
    v_t[:, cells] = speed.T
    h_t[:, cells] = layer.T
    k = lighter.astype(F32)
    hi = jnp.floor(k * (1 / 15.0) + (1 / 30.0))
    hi_t[:, cells] = hi.astype(BF16).T
    lo_t[:, cells] = (k - hi * 15.0).astype(BF16).T
    part = layer.astype(F32) * (share.astype(F32) * (1 / 64.0))
    q = part.astype(BF16)
    q_t[:, cells] = q.T
    e_t[:, cells] = (part - q.astype(F32)).astype(BF16).T


def group_sums(turned, rows, diagonal):
    total = None
    for start in range(0, 1024, 256):
        cells = slice(start, start + 256)
        v, h, hi, lo, q, e = (ref[rows, cells] for ref in turned)
        zero = jnp.zeros_like(v)
        a = jnp.concatenate([jnp.where(hi == float(x), v, zero) for x in range(16)], axis=0)
        b, f = [], []
        below = zero
        for x in range(15):
            here = lo == float(x)
            b.append(jnp.where(here, q, below))
            f.append(jnp.where(here, e, zero))
            below = jnp.where(here, h, below)
        b = jnp.concatenate(b + [below], axis=0)
        f = jnp.concatenate(f + [zero], axis=0)
        part = lax.dot_general(
            jnp.concatenate([a, a], axis=1),
            jnp.concatenate([b, f], axis=1),
            NT,
            preferred_element_type=F32,
        )
        total = part if total is None else total + part
    return jnp.where(diagonal[None], total.reshape(16, 16, 256), 0.0).sum(1)


def arrange(sums, width, units, unit_of):
    lane = lax.broadcasted_iota(jnp.int32, (16, 128), 1)
    slot = [[None, None] for _ in range(16)]
    for half in range(2):
        for part in range(2):
            x = [sums[half * 8 + g, :, part * 128 : part * 128 + 128] for g in range(8)]
            for d in (4, 2, 1):
                high = (lane & (16 * d)) != 0
                y = list(x)
                for i in range(8):
                    if i & d == 0:
                        y[i] = jnp.where(high, pltpu.roll(x[i + d], 16 * d, 1), x[i])
                        y[i + d] = jnp.where(high, x[i + d], pltpu.roll(x[i], 128 - 16 * d, 1))
                x = y
            for i in range(8):
                slot[part * 8 + i][half] = x[i]
    hi = lax.broadcasted_iota(jnp.int32, (16, 128), 0)
    for half in range(2):
        whole = slot[15][half]
        run = whole
        for d in (1, 2, 4, 8):
            run = run + jnp.where(hi >= d, pltpu.roll(run, d, 0), 0.0)
        offset = run - whole
        z = width[:, half * 128 : half * 128 + 128]
        for x in range(15):
            y = (slot[x][half] + offset) * z
            for cut in range(2):
                units[unit_of(cut, half), pl.ds(x, 8, stride=15), :] = y[cut * 8 : cut * 8 + 8]


def kernel(comm, v_hbm, h_hbm, k_hbm, w_hbm, width, psi_hbm, mean_ref, var_ref, *scratch):
    (raw_v, raw_h, raw_k, raw_w), scratch = scratch[:4], scratch[4:]
    even, odd, scratch = scratch[:6], scratch[6:12], scratch[12:]
    (sums, send, got_1, mid, got_2, own, pad, stat, got_3, read_sem, write_sem) = scratch[:11]
    (s1, r1, s2, r2, s3, r3, s4, r4, s5, r5) = scratch[11:]
    if comm:
        tm, lon, cls = lax.axis_index("tm"), lax.axis_index("lon"), lax.axis_index("cls")
    else:
        tm, lon, cls = jnp.int32(0), jnp.int32(0), jnp.int32(0)
    zz, xx, yy = lon // 8, (lon // 2) % 4, lon % 2
    n_own = 8

    def read(s, slot):
        return [
            pltpu.make_async_copy(src.at[cls * n_own + s], dst.at[slot], read_sem.at[slot, i])
            for i, (src, dst) in enumerate(
                zip((v_hbm, h_hbm, k_hbm, w_hbm), (raw_v, raw_h, raw_k, raw_w))
            )
        ]

    def lon_of(p, a, b, y):
        return a * 8 + b * 2 + y if p else b * 8 + a * 2 + y

    def spot(p):
        return (zz, xx) if p else (xx, zz)

    def first(p, s, rel):
        a, b = spot(p)
        to = (a + rel) % 4
        return pltpu.make_async_remote_copy(
            src_ref=send.at[s, to], dst_ref=got_1.at[s, 3 - rel], send_sem=s1.at[s, rel - 1],
            recv_sem=r1.at[s, 3 - rel], device_id={"lon": lon_of(p, to, b, yy)}, device_id_type=MESH)

    def second(p, s, rel):
        a, b = spot(p)
        to = (b * 2 + yy + rel) % 8
        return pltpu.make_async_remote_copy(
            src_ref=mid.at[s, pl.ds(pl.multiple_of(to * 16, 16), 16)], dst_ref=got_2.at[s, 7 - rel],
            send_sem=s2.at[s, rel - 1], recv_sem=r2.at[s, 7 - rel],
            device_id={"lon": lon_of(p, a, to // 2, to % 2)}, device_id_type=MESH)

    def unit_at(p, a):
        home = (cls + a // 2) % 2
        return home * n_own, a % 2

    def third(p, s, rel):
        a, b = spot(p)
        me = b * 2 + yy
        to = (me + rel) % 8
        rows = pl.ds(pl.multiple_of(me * 16, 16), 16)
        return pltpu.make_async_remote_copy(
            src_ref=own.at[s], dst_ref=pad.at[cls * n_own + s, a % 2, rows],
            send_sem=s3.at[s, rel], recv_sem=r3.at[s, (8 - rel) % 8],
            device_id={"lon": lon_of(p, a, to // 2, to % 2), "cls": (cls + a // 2) % 2},
            device_id_type=MESH)

    def third_got(p, s, rel):
        a, b = spot(p)
        base, half = unit_at(p, a)
        frm = (b * 2 + yy + rel) % 8
        rows = pl.ds(pl.multiple_of(frm * 16, 16), 16)
        dst = pad.at[base + s, half, rows]
        return pltpu.make_async_remote_copy(
            src_ref=own.at[s], dst_ref=dst, send_sem=s3.at[s, rel], recv_sem=r3.at[s, rel],
            device_id={"lon": lon_of(p, a, frm // 2, frm % 2), "cls": (cls + a // 2) % 2},
            device_id_type=MESH)

    def fourth(p, s, rel):
        a, b = spot(p)
        base, half = unit_at(p, a)
        return pltpu.make_async_remote_copy(
            src_ref=pad.at[base + s, half], dst_ref=pad.at[base + s, half], send_sem=s4.at[s, rel - 1],
            recv_sem=r4.at[s, 3 - rel], device_id={"lon": lon_of(p, (a + rel) % 4, b, yy)},
            device_id_type=MESH)

    def fourth_got(p, s, rel):
        a, b = spot(p)
        frm = (a + rel) % 4
        base, half = unit_at(p, frm)
        dst = pad.at[base + s, half]
        return pltpu.make_async_remote_copy(
            src_ref=dst, dst_ref=dst, send_sem=s4.at[s, rel - 1], recv_sem=r4.at[s, rel - 1],
            device_id={"lon": lon_of(p, frm, b, yy)}, device_id_type=MESH)

    def write(s):
        return [
            pltpu.make_async_copy(
                pad.at[base + s, half, pl.ds(0, C // 2)],
                psi_hbm.at[base + s, :, pl.ds(half * 128, 128)],
                write_sem.at[s, base // 4 + half])
            for base in (0, n_own) for half in (0, 1)
        ]

    def start_1(p, s):
        for rel in (1, 2, 3):
            first(p, s, rel).start()

    def start_2(p, s):
        a, _ = spot(p)
        for rel in (1, 2, 3):
            first(p, s, 4 - rel).wait_recv()
        mid[s] = send[s, a] + got_1[s, 0] + got_1[s, 1] + got_1[s, 2]
        for rel in range(1, 8):
            second(p, s, rel).start()

    def start_3(p, s):
        a, b = spot(p)
        me = b * 2 + yy
        rows = pl.ds(pl.multiple_of(me * 16, 16), 16)
        for rel in range(1, 8):
            second(p, s, 8 - rel).wait_recv()
        total = mid[s, rows]
        for i in range(7):
            total = total + got_2[s, i]
        own[s] = total

        @pl.when(a < 2)
        def _():
            pad[cls * n_own + s, a % 2, rows] = total

        @pl.when(a >= 2)
        def _():
            third(p, s, 0).start()

        for rel in range(1, 8):
            third(p, s, rel).start()

    def start_4(p, s):
        a, _ = spot(p)

        @pl.when(a >= 2)
        def _():
            third_got(p, s, 0).wait_recv()

        for rel in range(1, 8):
            third_got(p, s, rel).wait_recv()
        for rel in (1, 2, 3):
            fourth(p, s, rel).start()

    def take(s):
        for half in range(2):
            one, two = stat[half, 0], stat[half, 1]
            for base in (0, n_own):
                x = pad[base + s, half]
                one = one + x
                two = two + x * x
            stat[half, 0] = one
            stat[half, 1] = two

    def finish(p, s):
        for rel in (1, 2, 3):
            fourth_got(p, s, rel).wait_recv()
        for copy in write(s):
            copy.start()
        take(s)

    def drain(p, s):
        a, _ = spot(p)
        for rel in (1, 2, 3):
            first(p, s, rel).wait_send()
            fourth(p, s, rel).wait_send()
        for rel in range(1, 8):
            second(p, s, rel).wait_send()
            third(p, s, rel).wait_send()

        @pl.when(a >= 2)
        def _():
            third(p, s, 0).wait_send()

        for copy in write(s):
            copy.wait()

    barrier = None
    if comm:
        barrier = pltpu.get_barrier_semaphore()
        def greet(to, where):
            pl.semaphore_signal(barrier, inc=1, device_id=where, device_id_type=MESH)

        for y in range(2):
            for i in range(4):
                for near in range(2):
                    group = (cls + near) % 2
                    row = {"lon": ((zz + i) % 4) * 8 + xx * 2 + (yy + y) % 2, "cls": group}
                    if near or i or y:
                        greet(None, row)
                    if i:
                        greet(None, {"lon": zz * 8 + ((xx + i) % 4) * 2 + (yy + y) % 2, "cls": group})
        greet(None, {"tm": 1 - tm})
    n_greet = 2 * 2 * 4 - 1 + 2 * 2 * 3 + 1

    lane = lax.broadcasted_iota(jnp.int32, (16, 256), 1)
    row = lax.broadcasted_iota(jnp.int32, (16, 256), 0)
    diagonal = (lane & 15) == row
    raws = [[ref.at[slot] for ref in (raw_v, raw_h, raw_k, raw_w)] for slot in range(2)]

    for copy in read(0, 0):
        copy.start()
    for copy in read(1, 1):
        copy.start()
    stat[...] = jnp.zeros_like(stat)
    for copy in read(0, 0):
        copy.wait()

    def prologue(chunk, carry):
        prepare(raws[0], even, chunk)
        return carry

    lax.fori_loop(0, 4, prologue, 0)

    def compute(s, p):
        here, there = (odd, even) if p else (even, odd)

        @pl.when(s + 2 < n_own)
        def _():
            for copy in read(s + 2, p):
                copy.start()

        @pl.when(s + 1 < n_own)
        def _():
            for copy in read(s + 1, 1 - p):
                copy.wait()

        def step(j, carry):
            for c in range(GROUPS // 4):
                prepare(raws[1 - p], there, j * (GROUPS // 4) + c)
            for g in range(GROUPS):
                at = j * GROUPS + g
                rows = pl.ds(pl.multiple_of(at * 16, 16), 16)
                sums[at] = group_sums(here, rows, diagonal)
            return carry

        lax.fori_loop(0, 16 // GROUPS, step, 0)
        units = send.at[s]
        for u in range(4):
            units[u, pl.ds(C // 2, 8), :] = jnp.zeros((8, 128), F32)
        arrange(sums, width[...], units, lambda cut, half: ((cls + cut) % 2) * 2 + half)

    def pair(t, carry):
        for p in range(2):
            s = 2 * t + p
            compute(s, p)
            if not comm:
                continue
            if p == 0:
                @pl.when(t == 0)
                def _():
                    pl.semaphore_wait(barrier, n_greet)
            start_1(p, s)

            def guard(least, go, q, back):
                if least <= p:
                    go(q, s - back)
                else:
                    @pl.when(s >= least)
                    def _():
                        go(q, s - back)

            guard(1, start_2, 1 - p, 1)
            guard(2, start_3, p, 2)
            guard(3, start_4, 1 - p, 3)
            guard(4, finish, p, 4)
        return carry

    lax.fori_loop(0, n_own // 2, pair, 0)
    if comm:
        start_2(1, 7)
        start_3(0, 6)
        start_4(1, 5)
        finish(0, 4)
        start_3(1, 7)
        start_4(0, 6)
        finish(1, 5)
        start_4(1, 7)
        finish(0, 6)
        finish(1, 7)
        swap = pltpu.make_async_remote_copy(
            src_ref=stat.at[1 - tm], dst_ref=got_3, send_sem=s5, recv_sem=r5,
            device_id={"tm": 1 - tm}, device_id_type=MESH)
        swap.start()
        def drains(t, carry):
            drain(0, 2 * t)
            drain(1, 2 * t + 1)
            return carry
        lax.fori_loop(0, n_own // 2, drains, 0)
        swap.wait()
    else:
        for s in range(8):
            pad[s, 0] = send[s, 0]
            pad[s, 1] = send[s, 1]
            pad[s + 8, 0] = send[s, 2]
            pad[s + 8, 1] = send[s, 3]
            for copy in write(s):
                copy.start()
            for copy in write(s):
                copy.wait()
        got_3[...] = jnp.zeros_like(got_3)
    count = 32.0
    mean = (stat[tm, 0] + got_3[0]) / count
    var = (stat[tm, 1] + got_3[1]) / count - mean * mean
    mean_ref[...] = pltpu.roll(mean, (128 - lon * 4) % 128, 1)[: C // 2, :4]
    var_ref[...] = pltpu.roll(var, (128 - lon * 4) % 128, 1)[: C // 2, :4]


def overturning(v, h, k, w, width, comm=True):
    dma = pltpu.SemaphoreType.DMA
    hbm = pl.BlockSpec(memory_space=pl.ANY)
    vmem = pl.BlockSpec(memory_space=pltpu.VMEM)
    scratch = [pltpu.VMEM((2, 32, 32, 256), d) for d in (BF16, BF16, jnp.int32, jnp.int32)]
    scratch += [pltpu.VMEM((256, 1024), BF16)] * 12
    scratch += [
        pltpu.VMEM((16, 16, 256), F32),
        pltpu.VMEM((8, 4, 128, 128), F32),
        pltpu.VMEM((8, 3, 128, 128), F32),
        pltpu.VMEM((8, 128, 128), F32),
        pltpu.VMEM((8, 7, 16, 128), F32),
        pltpu.VMEM((8, 16, 128), F32),
        pltpu.VMEM((16, 2, 128, 128), F32),
        pltpu.VMEM((2, 2, 128, 128), F32),
        pltpu.VMEM((2, 128, 128), F32),
        dma((2, 4)), dma((8, 4)),
        dma((8, 3)), dma((8, 3)), dma((8, 7)), dma((8, 7)),
        dma((8, 8)), dma((8, 8)), dma((8, 3)), dma((8, 3)), dma, dma,
    ]
    return pl.pallas_call(
        functools.partial(kernel, comm),
        in_specs=[hbm] * 4 + [vmem],
        out_specs=(hbm, vmem, vmem),
        out_shape=(
            jax.ShapeDtypeStruct((16, C // 2, 256), F32),
            jax.ShapeDtypeStruct((C // 2, 4), F32),
            jax.ShapeDtypeStruct((C // 2, 4), F32),
        ),
        scratch_shapes=scratch,
        compiler_params=pltpu.CompilerParams(
            vmem_limit_bytes=56 * 2**20,
            **(dict(collective_id=0, has_side_effects=True) if comm else {}),
        ),
        name="overturning",
    )(v, h, k, w, width)


def shards(velocity, thickness, class_index, layer_weight, zonal_width):
    return overturning(velocity, thickness, class_index, layer_weight, zonal_width.reshape(1, -1))


def solution(mesh):
    cells = P("tm", "lon", None, None)
    in_specs = (cells, cells, cells, cells, P())
    out_specs = (P("tm", "cls", None), P("cls", ("tm", "lon")), P("cls", ("tm", "lon")))
    return jax.shard_map(shards, mesh=mesh, in_specs=in_specs, out_specs=out_specs, check_vma=False)
```

```python
import functools
import jax
import jax.numpy as jnp
from jax import lax
from jax.experimental import pallas as pl
from jax.experimental.pallas import tpu as pltpu
from jax.sharding import PartitionSpec as P

C = 240
GROUPS = 8
LAST = 8
NT = (((1,), (1,)), ((), ()))
MESH = pl.DeviceIdType.MESH
F32, BF16 = jnp.float32, jnp.bfloat16


def prepare(raw, turned, chunk):
    lons = pl.ds(chunk * 8, 8)
    cells = pl.ds(pl.multiple_of(chunk * 256, 256), 256)
    speed, layer, lighter, share = (ref[lons].reshape(256, 256) for ref in raw)
    v_t, h_t, hi_t, lo_t, q_t, e_t = turned
    v_t[:, cells] = speed.T
    h_t[:, cells] = layer.T
    k = lighter.astype(F32)
    hi = jnp.floor(k * (1 / 15.0) + (1 / 30.0))
    hi_t[:, cells] = hi.astype(BF16).T
    lo_t[:, cells] = (k - hi * 15.0).astype(BF16).T
    part = layer.astype(F32) * (share.astype(F32) * (1 / 64.0))
    q = part.astype(BF16)
    q_t[:, cells] = q.T
    e_t[:, cells] = (part - q.astype(F32)).astype(BF16).T


def group_sums(turned, rows, diagonal):
    total = None
    for start in range(0, 1024, 256):
        cells = slice(start, start + 256)
        v, h, hi, lo, q, e = (ref[rows, cells] for ref in turned)
        zero = jnp.zeros_like(v)
        a = jnp.concatenate([jnp.where(hi == float(x), v, zero) for x in range(16)], axis=0)
        b, f = [], []
        below = zero
        for x in range(15):
            here = lo == float(x)
            b.append(jnp.where(here, q, below))
            f.append(jnp.where(here, e, zero))
            below = jnp.where(here, h, below)
        b = jnp.concatenate(b + [below], axis=0)
        f = jnp.concatenate(f + [zero], axis=0)
        part = lax.dot_general(
            jnp.concatenate([a, a], axis=1),
            jnp.concatenate([b, f], axis=1),
            NT,
            preferred_element_type=F32,
        )
        total = part if total is None else total + part
    return jnp.where(diagonal[None], total.reshape(16, 16, 256), 0.0).sum(1)


def arrange(sums, width, units, slot_of):
    lane = lax.broadcasted_iota(jnp.int32, (16, 128), 1)
    slot = []
    for part in range(2):
        x = [sums[g, :, part * 128 : part * 128 + 128] for g in range(8)]
        for d in (4, 2, 1):
            high = (lane & (16 * d)) != 0
            y = list(x)
            for i in range(8):
                if i & d == 0:
                    y[i] = jnp.where(high, pltpu.roll(x[i + d], 16 * d, 1), x[i])
                    y[i + d] = jnp.where(high, x[i + d], pltpu.roll(x[i], 128 - 16 * d, 1))
            x = y
        slot += x
    hi = lax.broadcasted_iota(jnp.int32, (16, 128), 0)
    run = slot[15]
    for d in (1, 2, 4, 8):
        run = run + jnp.where(hi >= d, pltpu.roll(run, d, 0), 0.0)
    offset = run - slot[15]
    for x in range(15):
        y = (slot[x] + offset) * width
        for cut in range(2):
            units[slot_of(cut), pl.ds(x, 8, stride=15), :] = y[cut * 8 : cut * 8 + 8]


def kernel(comm, v_hbm, h_hbm, k_hbm, w_hbm, width, psi_hbm, mean_ref, var_ref, *scratch):
    (raw_v, raw_h, raw_k, raw_w), scratch = scratch[:4], scratch[4:]
    even, odd, scratch = scratch[:6], scratch[6:12], scratch[12:]
    (sums, send, got_1, mid, got_2, own, pad, stat, got_3, read_sem, write_sem) = scratch[:11]
    (s1, r1, s2, r2, s3, r3, s4, r4, s5, r5) = scratch[11:]
    if comm:
        tm, lon, cls = lax.axis_index("tm"), lax.axis_index("lon"), lax.axis_index("cls")
    else:
        tm, lon, cls = jnp.int32(0), jnp.int32(0), jnp.int32(0)
    zz, xx, yy = lon // 8, (lon // 2) % 4, lon % 2
    n_own = 8

    def read(s, slot):
        return [
            pltpu.make_async_copy(src.at[cls * n_own + s], dst.at[slot], read_sem.at[slot, i])
            for i, (src, dst) in enumerate(
                zip((v_hbm, h_hbm, k_hbm, w_hbm), (raw_v, raw_h, raw_k, raw_w))
            )
        ]

    spots = ((xx, zz), (zz, xx))
    cols, col_lon, place, place_lon = [], [], [], []
    for p, (a, b) in enumerate(spots):
        step_a, step_b = (8, 2) if p else (2, 8)
        near = [a] + [(a + rel) % 4 for rel in (1, 2, 3)]
        cols.append(near)
        col_lon.append([c * step_a + b * step_b + yy for c in near])
        me = b * 2 + yy
        near = [me] + [(me + rel) % 8 for rel in range(1, 8)]
        place.append(near)
        place_lon.append([a * step_a + (n // 2) * step_b + n % 2 for n in near])
    home = [(cls + a // 2) % 2 for a, _ in spots]

    def size(job):
        return 128 if job[3] is None else 64

    def unit_of(job, col):
        half = job[3]
        if half is None:
            return col, 0, col % 2
        return (col // 2) * 2 + half, (col % 2) * 64, half

    def base(job, n):
        return 0 if job[3] is None else job[3] * n

    def span(start, n):
        return pl.ds(start if isinstance(start, int) else pl.multiple_of(start, 8), n)

    def first(job, rel):
        i, p, s, _ = job
        n = size(job)
        u, r, _ = unit_of(job, cols[p][rel])
        return pltpu.make_async_remote_copy(
            src_ref=send.at[s, u, span(r, n)], dst_ref=got_1.at[s, 3 - rel, span(base(job, 64), n)],
            send_sem=s1.at[i, rel - 1], recv_sem=r1.at[i, 3 - rel],
            device_id={"lon": col_lon[p][rel]}, device_id_type=MESH)

    def second(job, rel):
        i, p, s, _ = job
        n = size(job) // 8
        return pltpu.make_async_remote_copy(
            src_ref=mid.at[s, span(base(job, 64) + place[p][rel] * n, n)],
            dst_ref=got_2.at[s, 7 - rel, span(base(job, 8), n)],
            send_sem=s2.at[i, rel - 1], recv_sem=r2.at[i, 7 - rel],
            device_id={"lon": place_lon[p][rel]}, device_id_type=MESH)

    def target(job, group, rel):
        _, p, s, _ = job
        n = size(job) // 8
        _, r, half = unit_of(job, cols[p][0])
        return pad.at[group * n_own + s, half, span(r + place[p][rel] * n, n)]

    def third(job, rel):
        i, p, s, _ = job
        return pltpu.make_async_remote_copy(
            src_ref=own.at[s, span(base(job, 8), size(job) // 8)], dst_ref=target(job, cls, 0),
            send_sem=s3.at[i, rel], recv_sem=r3.at[i, (8 - rel) % 8],
            device_id={"lon": place_lon[p][rel], "cls": home[p]}, device_id_type=MESH)

    def third_got(job, rel):
        i, p, s, _ = job
        return pltpu.make_async_remote_copy(
            src_ref=own.at[s, span(base(job, 8), size(job) // 8)], dst_ref=target(job, home[p], rel),
            send_sem=s3.at[i, rel], recv_sem=r3.at[i, rel],
            device_id={"lon": place_lon[p][rel], "cls": home[p]}, device_id_type=MESH)

    def spread(job, rel):
        _, p, s, _ = job
        col = cols[p][rel]
        _, r, half = unit_of(job, col)
        return pad.at[(cls + col // 2) % 2 * n_own + s, half, span(r, size(job))]

    def fourth(job, rel):
        i, p, _, _ = job
        return pltpu.make_async_remote_copy(
            src_ref=spread(job, 0), dst_ref=spread(job, 0), send_sem=s4.at[i, rel - 1],
            recv_sem=r4.at[i, 3 - rel], device_id={"lon": col_lon[p][rel]}, device_id_type=MESH)

    def fourth_got(job, rel):
        i, p, _, _ = job
        dst = spread(job, rel)
        return pltpu.make_async_remote_copy(
            src_ref=dst, dst_ref=dst, send_sem=s4.at[i, rel - 1], recv_sem=r4.at[i, rel - 1],
            device_id={"lon": col_lon[p][rel]}, device_id_type=MESH)

    def write(s):
        return [
            pltpu.make_async_copy(
                pad.at[base + s, half, pl.ds(0, C // 2)],
                psi_hbm.at[base + s, :, pl.ds(half * 128, 128)],
                write_sem.at[s, base // 4 + half])
            for base in (0, n_own) for half in (0, 1)
        ]

    def start_1(job):
        for rel in (1, 2, 3):
            first(job, rel).start()

    def start_2(job):
        _, p, s, _ = job
        n = size(job)
        u, r, _ = unit_of(job, cols[p][0])
        rows = span(base(job, 64), n)
        for rel in (1, 2, 3):
            first(job, rel).wait_recv()
        mid[s, rows] = send[s, u, span(r, n)] + got_1[s, 0, rows] + got_1[s, 1, rows] + got_1[s, 2, rows]
        for rel in range(1, 8):
            second(job, rel).start()

    def start_3(job):
        _, p, s, _ = job
        n = size(job) // 8
        rows = span(base(job, 8), n)
        for rel in range(1, 8):
            second(job, rel).wait_recv()
        total = mid[s, span(base(job, 64) + place[p][0] * n, n)]
        for i in range(7):
            total = total + got_2[s, i, rows]
        own[s, rows] = total

        @pl.when(cols[p][0] < 2)
        def _():
            target(job, cls, 0)[...] = total

        @pl.when(cols[p][0] >= 2)
        def _():
            third(job, 0).start()

        for rel in range(1, 8):
            third(job, rel).start()

    def start_4(job):
        p = job[1]

        @pl.when(cols[p][0] >= 2)
        def _():
            third_got(job, 0).wait_recv()

        for rel in range(1, 8):
            third_got(job, rel).wait_recv()
        for rel in (1, 2, 3):
            fourth(job, rel).start()

    def take(s):
        for half in range(2):
            one, two = stat[half, 0], stat[half, 1]
            for base in (0, n_own):
                x = pad[base + s, half]
                one = one + x
                two = two + x * x
            stat[half, 0] = one
            stat[half, 1] = two

    def finish(job):
        for rel in (1, 2, 3):
            fourth_got(job, rel).wait_recv()
        if job[0] is not LAST - 1:
            for copy in write(job[2]):
                copy.start()
            take(job[2])

    def drain(job):
        for rel in (1, 2, 3):
            first(job, rel).wait_send()
            fourth(job, rel).wait_send()
        for rel in range(1, 8):
            second(job, rel).wait_send()
            third(job, rel).wait_send()

        @pl.when(cols[job[1]][0] >= 2)
        def _():
            third(job, 0).wait_send()

        if job[0] is not LAST - 1:
            for copy in write(job[2]):
                copy.wait()

    def whole(q, s):
        return (s, q, s, None)

    ends = ((LAST - 1, 1, 7, 0), (LAST, 0, 7, 1))

    barrier = None
    if comm:
        barrier = pltpu.get_barrier_semaphore()
        def greet(to, where):
            pl.semaphore_signal(barrier, inc=1, device_id=where, device_id_type=MESH)

        for y in range(2):
            for i in range(4):
                for near in range(2):
                    group = (cls + near) % 2
                    row = {"lon": ((zz + i) % 4) * 8 + xx * 2 + (yy + y) % 2, "cls": group}
                    if near or i or y:
                        greet(None, row)
                    if i:
                        greet(None, {"lon": zz * 8 + ((xx + i) % 4) * 2 + (yy + y) % 2, "cls": group})
        greet(None, {"tm": 1 - tm})
    n_greet = 2 * 2 * 4 - 1 + 2 * 2 * 3 + 1

    lane = lax.broadcasted_iota(jnp.int32, (16, 256), 1)
    row = lax.broadcasted_iota(jnp.int32, (16, 256), 0)
    diagonal = (lane & 15) == row
    raws = [[ref.at[slot] for ref in (raw_v, raw_h, raw_k, raw_w)] for slot in range(2)]

    for copy in read(0, 0):
        copy.start()
    for copy in read(1, 1):
        copy.start()
    stat[...] = jnp.zeros_like(stat)
    for copy in read(0, 0):
        copy.wait()

    def pad_rows(s, carry):
        for u in range(4):
            send[s, u, pl.ds(C // 2, 8), :] = jnp.zeros((8, 128), F32)
        return carry

    lax.fori_loop(0, n_own, pad_rows, 0)

    def prologue(chunk, carry):
        prepare(raws[0], even, chunk)
        return carry

    lax.fori_loop(0, 4, prologue, 0)

    def compute(s, p):
        here, there = (odd, even) if p else (even, odd)

        @pl.when(s + 2 < n_own)
        def _():
            for copy in read(s + 2, p):
                copy.start()

        @pl.when(s + 1 < n_own)
        def _():
            for copy in read(s + 1, 1 - p):
                copy.wait()

        def step(j, carry):
            for c in range(GROUPS // 4):
                prepare(raws[1 - p], there, j * (GROUPS // 4) + c)
            for g in range(GROUPS):
                rows = pl.ds(pl.multiple_of((j * GROUPS + g) * 16, 16), 16)
                sums[g] = group_sums(here, rows, diagonal)
            arrange(sums, width[pl.ds(j, 1), :], send.at[s], lambda cut: ((cls + cut) % 2) * 2 + j)
            if comm and p == 1:
                @pl.when((s == n_own - 1) & (j == 0))
                def _():
                    start_1(ends[0])
                    start_2(whole(0, 6))
                    start_3(whole(1, 5))
                    start_4(whole(0, 4))
                    finish(whole(1, 3))
            return carry

        lax.fori_loop(0, 16 // GROUPS, step, 0)

    def pair(t, carry):
        for p in range(2):
            s = 2 * t + p
            compute(s, p)
            if not comm:
                continue

            def advance():
                start_1(whole(p, s))
                for least, go, q in ((1, start_2, 1 - p), (2, start_3, p), (3, start_4, 1 - p), (4, finish, p)):
                    if least <= p:
                        go(whole(q, s - least))
                    else:
                        @pl.when(s >= least)
                        def _(go=go, q=q, least=least):
                            go(whole(q, s - least))

            if p == 0:
                @pl.when(t == 0)
                def _():
                    pl.semaphore_wait(barrier, n_greet)
                advance()
            else:
                pl.when(s < n_own - 1)(advance)
        return carry

    lax.fori_loop(0, n_own // 2, pair, 0)
    if comm:
        early, late = ends
        start_1(late)
        start_2(early)
        start_3(whole(0, 6))
        start_4(whole(1, 5))
        finish(whole(0, 4))
        start_2(late)
        start_3(early)
        start_4(whole(0, 6))
        finish(whole(1, 5))
        start_3(late)
        start_4(early)
        finish(whole(0, 6))
        start_4(late)
        finish(early)
        finish(late)
        swap = pltpu.make_async_remote_copy(
            src_ref=stat.at[1 - tm], dst_ref=got_3, send_sem=s5, recv_sem=r5,
            device_id={"tm": 1 - tm}, device_id_type=MESH)
        swap.start()

        def drains(t, carry):
            drain(whole(0, 2 * t))
            drain(whole(1, 2 * t + 1))
            return carry

        lax.fori_loop(0, n_own // 2 - 1, drains, 0)
        drain(whole(0, 6))
        for job in ends:
            drain(job)
        swap.wait()
    else:
        for s in range(8):
            pad[s, 0] = send[s, 0]
            pad[s, 1] = send[s, 1]
            pad[s + 8, 0] = send[s, 2]
            pad[s + 8, 1] = send[s, 3]
        for s in (0, 7):
            for copy in write(s):
                copy.start()
            for copy in write(s):
                copy.wait()
        got_3[...] = jnp.zeros_like(got_3)
    count = 32.0
    mean = (stat[tm, 0] + got_3[0]) / count
    var = (stat[tm, 1] + got_3[1]) / count - mean * mean
    mean_ref[...] = pltpu.roll(mean, (128 - lon * 4) % 128, 1)[: C // 2, :4]
    var_ref[...] = pltpu.roll(var, (128 - lon * 4) % 128, 1)[: C // 2, :4]


def overturning(v, h, k, w, width, comm=True):
    dma = pltpu.SemaphoreType.DMA
    hbm = pl.BlockSpec(memory_space=pl.ANY)
    vmem = pl.BlockSpec(memory_space=pltpu.VMEM)
    scratch = [pltpu.VMEM((2, 32, 32, 256), d) for d in (BF16, BF16, jnp.int32, jnp.int32)]
    scratch += [pltpu.VMEM((256, 1024), BF16)] * 12
    scratch += [
        pltpu.VMEM((GROUPS, 16, 256), F32),
        pltpu.VMEM((8, 4, 128, 128), F32),
        pltpu.VMEM((8, 3, 128, 128), F32),
        pltpu.VMEM((8, 128, 128), F32),
        pltpu.VMEM((8, 7, 16, 128), F32),
        pltpu.VMEM((8, 16, 128), F32),
        pltpu.VMEM((16, 2, 128, 128), F32),
        pltpu.VMEM((2, 2, 128, 128), F32),
        pltpu.VMEM((2, 128, 128), F32),
        dma((2, 4)), dma((8, 4)),
        dma((9, 3)), dma((9, 3)), dma((9, 7)), dma((9, 7)),
        dma((9, 8)), dma((9, 8)), dma((9, 3)), dma((9, 3)), dma, dma,
    ]
    return pl.pallas_call(
        functools.partial(kernel, comm),
        in_specs=[hbm] * 4 + [vmem],
        out_specs=(hbm, vmem, vmem),
        out_shape=(
            jax.ShapeDtypeStruct((16, C // 2, 256), F32),
            jax.ShapeDtypeStruct((C // 2, 4), F32),
            jax.ShapeDtypeStruct((C // 2, 4), F32),
        ),
        scratch_shapes=scratch,
        compiler_params=pltpu.CompilerParams(
            vmem_limit_bytes=56 * 2**20,
            **(dict(collective_id=0, has_side_effects=True) if comm else {}),
        ),
        name="overturning",
    )(v, h, k, w, width)


def shards(velocity, thickness, class_index, layer_weight, zonal_width):
    return overturning(velocity, thickness, class_index, layer_weight, zonal_width.reshape(2, -1))


def solution(mesh):
    cells = P("tm", "lon", None, None)
    in_specs = (cells, cells, cells, cells, P())
    out_specs = (P("tm", "cls", None), P("cls", ("tm", "lon")), P("cls", ("tm", "lon")))
    return jax.shard_map(shards, mesh=mesh, in_specs=in_specs, out_specs=out_specs, check_vma=False)
```

```python
import functools
import jax
import jax.numpy as jnp
from jax import lax
from jax.experimental import pallas as pl
from jax.experimental.pallas import tpu as pltpu
from jax.sharding import PartitionSpec as P

C = 240
GROUPS = 8
LAST = 8
NT = (((1,), (1,)), ((), ()))
MESH = pl.DeviceIdType.MESH
F32, BF16 = jnp.float32, jnp.bfloat16


def prepare(raw, turned, chunk):
    lons = pl.ds(chunk * 8, 8)
    cells = pl.ds(pl.multiple_of(chunk * 256, 256), 256)
    speed, layer, lighter, share = (ref[lons].reshape(256, 256) for ref in raw)
    v_t, h_t, hi_t, lo_t, q_t, e_t = turned
    v_t[:, cells] = speed.T
    h_t[:, cells] = (layer * 64.0).T
    k = lighter.astype(F32)
    hi = (k * (1 / 15.0) + (129 - 7 / 15.0)).astype(BF16)
    hi_t[:, cells] = hi.T
    lo_t[:, cells] = (k.astype(BF16) - (hi - 129.0) * 15.0).T
    part = layer.astype(F32) * share.astype(F32)
    q = part.astype(BF16)
    q_t[:, cells] = q.T
    e_t[:, cells] = (part - q.astype(F32)).astype(BF16).T


def group_sums(turned, rows, diagonal):
    total = None
    for start in range(0, 1024, 256):
        cells = slice(start, start + 256)
        v, h, hi, lo, q, e = (ref[rows, cells] for ref in turned)
        zero = jnp.zeros_like(v)
        a = jnp.concatenate([jnp.where(hi == float(x + 129), v, zero) for x in range(16)], axis=0)
        b, f = [], []
        below = zero
        for x in range(15):
            here = lo == float(x)
            b.append(jnp.where(here, q, below))
            f.append(jnp.where(here, e, zero))
            below = jnp.where(here, h, below)
        b = jnp.concatenate(b + [below], axis=0)
        f = jnp.concatenate(f + [zero], axis=0)
        part = lax.dot_general(
            jnp.concatenate([b, f], axis=0), a, NT, preferred_element_type=F32
        )
        total = part if total is None else total + part
    total = total[:256] + total[256:]
    return jnp.where(diagonal[None], total.reshape(16, 16, 256), 0.0).sum(1)


def arrange(sums, width, units, slot_of):
    lane = lax.broadcasted_iota(jnp.int32, (16, 128), 1)
    offset = jnp.zeros((1, 128), F32)
    for part in range(2):
        x = [sums[g, :, part * 128 : part * 128 + 128] for g in range(8)]
        for d in (4, 2, 1):
            high = (lane & (16 * d)) != 0
            y = list(x)
            for i in range(8):
                if i & d == 0:
                    y[i] = jnp.where(high, pltpu.roll(x[i + d], 16 * d, 1), x[i])
                    y[i + d] = jnp.where(high, x[i + d], pltpu.roll(x[i], 128 - 16 * d, 1))
            x = y
        for i in range(8):
            units[slot_of(part), 15 * i : 15 * i + 16, :] = (x[i] + offset) * width
            offset = offset + x[i][15:16]


def kernel(comm, v_hbm, h_hbm, k_hbm, w_hbm, width, psi_hbm, total_ref, *scratch):
    (raw_v, raw_h, raw_k, raw_w), scratch = scratch[:4], scratch[4:]
    even, odd, scratch = scratch[:6], scratch[6:12], scratch[12:]
    (sums, send, got_1, mid, got_2, own, pad, stat, got_3, read_sem, quarter_sem, write_sem) = scratch[:12]
    (s1, r1, s2, r2, s3, r3, s4, r4, s5, r5) = scratch[12:]
    if comm:
        tm, lon, cls = lax.axis_index("tm"), lax.axis_index("lon"), lax.axis_index("cls")
    else:
        tm, lon, cls = jnp.int32(0), jnp.int32(0), jnp.int32(0)
    zz, xx, yy = lon // 8, (lon // 2) % 4, lon % 2
    n_own = 8

    def read(s, slot):
        return [
            pltpu.make_async_copy(src.at[cls * n_own + s], dst.at[slot], read_sem.at[slot, i])
            for i, (src, dst) in enumerate(
                zip((v_hbm, h_hbm, k_hbm, w_hbm), (raw_v, raw_h, raw_k, raw_w))
            )
        ]

    spots = ((xx, zz), (zz, xx))
    cols, col_lon, place, place_lon = [], [], [], []
    for p, (a, b) in enumerate(spots):
        step_a, step_b = (8, 2) if p else (2, 8)
        near = [a] + [(a + rel) % 4 for rel in (1, 2, 3)]
        cols.append(near)
        col_lon.append([c * step_a + b * step_b + yy for c in near])
        me = b * 2 + yy
        near = [me] + [(me + rel) % 8 for rel in range(1, 8)]
        place.append(near)
        place_lon.append([a * step_a + (n // 2) * step_b + n % 2 for n in near])
    home = [(cls + a // 2) % 2 for a, _ in spots]

    def size(job):
        return 128 if job[3] is None else 64

    def unit_of(job, col):
        half = job[3]
        return col, 0 if half is None else half * 64, col % 2

    def base(job, n):
        return 0 if job[3] is None else job[3] * n

    def span(start, n):
        return pl.ds(start if isinstance(start, int) else pl.multiple_of(start, 8), n)

    def first(job, rel):
        i, p, s, _ = job
        n = size(job)
        u, r, _ = unit_of(job, cols[p][rel])
        return pltpu.make_async_remote_copy(
            src_ref=send.at[s, u, span(r, n)], dst_ref=got_1.at[s, 3 - rel, span(base(job, 64), n)],
            send_sem=s1.at[i, rel - 1], recv_sem=r1.at[i, 3 - rel],
            device_id={"lon": col_lon[p][rel]}, device_id_type=MESH)

    def second(job, rel):
        i, p, s, _ = job
        n = size(job) // 8
        return pltpu.make_async_remote_copy(
            src_ref=mid.at[s, span(base(job, 64) + place[p][rel] * n, n)],
            dst_ref=got_2.at[s, 7 - rel, span(base(job, 8), n)],
            send_sem=s2.at[i, rel - 1], recv_sem=r2.at[i, 7 - rel],
            device_id={"lon": place_lon[p][rel]}, device_id_type=MESH)

    def target(job, group, rel):
        _, p, s, _ = job
        n = size(job) // 8
        _, r, half = unit_of(job, cols[p][0])
        return pad.at[group * n_own + s, half, span(r + place[p][rel] * n, n)]

    def third(job, rel):
        i, p, s, _ = job
        return pltpu.make_async_remote_copy(
            src_ref=own.at[s, span(base(job, 8), size(job) // 8)], dst_ref=target(job, cls, 0),
            send_sem=s3.at[i, rel], recv_sem=r3.at[i, (8 - rel) % 8],
            device_id={"lon": place_lon[p][rel], "cls": home[p]}, device_id_type=MESH)

    def third_got(job, rel):
        i, p, s, _ = job
        return pltpu.make_async_remote_copy(
            src_ref=own.at[s, span(base(job, 8), size(job) // 8)], dst_ref=target(job, home[p], rel),
            send_sem=s3.at[i, rel], recv_sem=r3.at[i, rel],
            device_id={"lon": place_lon[p][rel], "cls": home[p]}, device_id_type=MESH)

    def spread(job, rel):
        _, p, s, _ = job
        col = cols[p][rel]
        _, r, half = unit_of(job, col)
        return pad.at[(cls + col // 2) % 2 * n_own + s, half, span(r, size(job))]

    def fourth(job, rel):
        i, p, _, _ = job
        return pltpu.make_async_remote_copy(
            src_ref=spread(job, 0), dst_ref=spread(job, 0), send_sem=s4.at[i, rel - 1],
            recv_sem=r4.at[i, 3 - rel], device_id={"lon": col_lon[p][rel]}, device_id_type=MESH)

    def fourth_got(job, rel):
        i, p, _, _ = job
        dst = spread(job, rel)
        return pltpu.make_async_remote_copy(
            src_ref=dst, dst_ref=dst, send_sem=s4.at[i, rel - 1], recv_sem=r4.at[i, rel - 1],
            device_id={"lon": col_lon[p][rel]}, device_id_type=MESH)

    def write(s):
        return [
            pltpu.make_async_copy(
                pad.at[base + s, half],
                psi_hbm.at[base + s, half],
                write_sem.at[s, base // 4 + half])
            for base in (0, n_own) for half in (0, 1)
        ]

    def start_1(job):
        for rel in (1, 2, 3):
            first(job, rel).start()

    def start_2(job):
        _, p, s, _ = job
        n = size(job)
        u, r, _ = unit_of(job, cols[p][0])
        rows = span(base(job, 64), n)
        for rel in (1, 2, 3):
            first(job, rel).wait_recv()
        mid[s, rows] = send[s, u, span(r, n)] + got_1[s, 0, rows] + got_1[s, 1, rows] + got_1[s, 2, rows]
        for rel in range(1, 8):
            second(job, rel).start()

    def start_3(job):
        _, p, s, _ = job
        n = size(job) // 8
        rows = span(base(job, 8), n)
        for rel in range(1, 8):
            second(job, rel).wait_recv()
        total = mid[s, span(base(job, 64) + place[p][0] * n, n)]
        for i in range(7):
            total = total + got_2[s, i, rows]
        own[s, rows] = total

        @pl.when(cols[p][0] < 2)
        def _():
            target(job, cls, 0)[...] = total

        @pl.when(cols[p][0] >= 2)
        def _():
            third(job, 0).start()

        for rel in range(1, 8):
            third(job, rel).start()

    def start_4(job):
        p = job[1]

        @pl.when(cols[p][0] >= 2)
        def _():
            third_got(job, 0).wait_recv()

        for rel in range(1, 8):
            third_got(job, rel).wait_recv()
        for rel in (1, 2, 3):
            fourth(job, rel).start()

    def take(s):
        for half in range(2):
            one, two = stat[half, 0], stat[half, 1]
            for base in (0, n_own):
                x = pad[base + s, half]
                one = one + x
                two = two + x * x
            stat[half, 0] = one
            stat[half, 1] = two

    def finish(job):
        for rel in (1, 2, 3):
            fourth_got(job, rel).wait_recv()
        if job[0] is not LAST - 1:
            for copy in write(job[2]):
                copy.start()
            take(job[2])

    def drain(job):
        for rel in (1, 2, 3):
            first(job, rel).wait_send()
            fourth(job, rel).wait_send()
        for rel in range(1, 8):
            second(job, rel).wait_send()
            third(job, rel).wait_send()

        @pl.when(cols[job[1]][0] >= 2)
        def _():
            third(job, 0).wait_send()

        if job[0] is not LAST - 1:
            for copy in write(job[2]):
                copy.wait()

    def whole(q, s):
        return (s, q, s, None)

    ends = ((LAST - 1, 1, 7, 0), (LAST, 0, 7, 1))

    barrier = None
    if comm:
        barrier = pltpu.get_barrier_semaphore()
        def greet(to, where):
            pl.semaphore_signal(barrier, inc=1, device_id=where, device_id_type=MESH)

        for y in range(2):
            for i in range(4):
                for near in range(2):
                    group = (cls + near) % 2
                    row = {"lon": ((zz + i) % 4) * 8 + xx * 2 + (yy + y) % 2, "cls": group}
                    if near or i or y:
                        greet(None, row)
                    if i:
                        greet(None, {"lon": zz * 8 + ((xx + i) % 4) * 2 + (yy + y) % 2, "cls": group})
        greet(None, {"tm": 1 - tm})
    n_greet = 2 * 2 * 4 - 1 + 2 * 2 * 3 + 1

    lane = lax.broadcasted_iota(jnp.int32, (16, 256), 1)
    row = lax.broadcasted_iota(jnp.int32, (16, 256), 0)
    diagonal = (lane & 15) == row
    raws = [[ref.at[slot] for ref in (raw_v, raw_h, raw_k, raw_w)] for slot in range(2)]

    def quarter(chunk):
        lons = pl.ds(chunk * 8, 8)
        return [
            pltpu.make_async_copy(src.at[cls * n_own, lons], dst.at[0, lons], quarter_sem.at[chunk, i])
            for i, (src, dst) in enumerate(
                zip((v_hbm, h_hbm, k_hbm, w_hbm), (raw_v, raw_h, raw_k, raw_w))
            )
        ]

    for chunk in range(4):
        for copy in quarter(chunk):
            copy.start()
    for copy in read(1, 1):
        copy.start()
    stat[...] = jnp.zeros_like(stat)
    def pad_rows(s, carry):
        for u in range(4):
            send[s, u, pl.ds(C // 2, 8), :] = jnp.zeros((8, 128), F32)
        return carry

    lax.fori_loop(0, n_own, pad_rows, 0)

    def prologue(chunk, carry):
        for copy in quarter(chunk):
            copy.wait()
        prepare(raws[0], even, chunk)
        return carry

    lax.fori_loop(0, 4, prologue, 0)

    def compute(s, p):
        here, there = (odd, even) if p else (even, odd)

        @pl.when(s + 2 < n_own)
        def _():
            for copy in read(s + 2, p):
                copy.start()

        @pl.when(s + 1 < n_own)
        def _():
            for copy in read(s + 1, 1 - p):
                copy.wait()

        def step(j, carry):
            for c in range(GROUPS // 4):
                prepare(raws[1 - p], there, j * (GROUPS // 4) + c)
            for g in range(GROUPS):
                rows = pl.ds(pl.multiple_of((j * GROUPS + g) * 16, 16), 16)
                sums[j * GROUPS + g] = group_sums(here, rows, diagonal)
            return carry

        lax.fori_loop(0, 16 // GROUPS, step, 0)
        for j in range(2):
            arrange(sums.at[pl.ds(j * 8, 8)], width[j : j + 1, :], send.at[s], lambda cut: ((cls + cut) % 2) * 2 + j)

    def pair(t, carry):
        for p in range(2):
            s = 2 * t + p
            compute(s, p)
            if not comm:
                continue

            def advance():
                start_1(whole(p, s))
                for least, go, q in ((1, start_2, 1 - p), (2, start_3, p), (3, start_4, 1 - p), (4, finish, p)):
                    if least <= p:
                        go(whole(q, s - least))
                    else:
                        @pl.when(s >= least)
                        def _(go=go, q=q, least=least):
                            go(whole(q, s - least))

            if p == 0:
                @pl.when(t == 0)
                def _():
                    pl.semaphore_wait(barrier, n_greet)
                advance()
            else:
                pl.when(s < n_own - 1)(advance)
        return carry

    lax.fori_loop(0, n_own // 2, pair, 0)
    if comm:
        for job in ends:
            start_1(job)
        start_2(whole(0, 6))
        start_3(whole(1, 5))
        start_4(whole(0, 4))
        finish(whole(1, 3))
        for job in ends:
            start_2(job)
        start_3(whole(0, 6))
        start_4(whole(1, 5))
        finish(whole(0, 4))
        for job in ends:
            start_3(job)
        start_4(whole(0, 6))
        finish(whole(1, 5))
        for job in ends:
            start_4(job)
        finish(whole(0, 6))
        for job in ends:
            finish(job)
        swap = pltpu.make_async_remote_copy(
            src_ref=stat.at[1 - tm], dst_ref=got_3, send_sem=s5, recv_sem=r5,
            device_id={"tm": 1 - tm}, device_id_type=MESH)
        swap.start()

        def drains(t, carry):
            drain(whole(0, 2 * t))
            drain(whole(1, 2 * t + 1))
            return carry

        lax.fori_loop(0, n_own // 2 - 1, drains, 0)
        drain(whole(0, 6))
        for job in ends:
            drain(job)
        swap.wait()
    else:
        for s in range(8):
            pad[s, 0] = send[s, 0]
            pad[s, 1] = send[s, 1]
            pad[s + 8, 0] = send[s, 2]
            pad[s + 8, 1] = send[s, 3]
        for s in (0, 7):
            for copy in write(s):
                copy.start()
            for copy in write(s):
                copy.wait()
        got_3[...] = jnp.zeros_like(got_3)
    total_ref[...] = stat[tm] + got_3[...]


def finals(pad_hbm, total, psi_hbm, mean_ref, var_ref, sem):
    copies = [
        pltpu.make_async_copy(
            pad_hbm.at[s, half, pl.ds(0, C // 2)], psi_hbm.at[s, :, pl.ds(half * 128, 128)], sem.at[s, half]
        )
        for s in range(16)
        for half in range(2)
    ]
    for copy in copies:
        copy.start()
    mean = total[0] / 32.0
    var = total[1] / 32.0 - mean * mean
    shift = (128 - lax.axis_index("lon") * 4) % 128
    mean_ref[...] = pltpu.roll(mean, shift, 1).T[:4, : C // 2]
    var_ref[...] = pltpu.roll(var, shift, 1).T[:4, : C // 2]
    for copy in copies:
        copy.wait()


def overturning(v, h, k, w, width, comm=True):
    dma = pltpu.SemaphoreType.DMA
    hbm = pl.BlockSpec(memory_space=pl.ANY)
    vmem = pl.BlockSpec(memory_space=pltpu.VMEM)
    scratch = [pltpu.VMEM((2, 32, 32, 256), d) for d in (BF16, BF16, jnp.int32, jnp.int32)]
    scratch += [pltpu.VMEM((256, 1024), BF16)] * 12
    scratch += [
        pltpu.VMEM((16, 16, 256), F32),
        pltpu.VMEM((8, 4, 128, 128), F32),
        pltpu.VMEM((8, 3, 128, 128), F32),
        pltpu.VMEM((8, 128, 128), F32),
        pltpu.VMEM((8, 7, 16, 128), F32),
        pltpu.VMEM((8, 16, 128), F32),
        pltpu.VMEM((16, 2, 128, 128), F32),
        pltpu.VMEM((2, 2, 128, 128), F32),
        pltpu.VMEM((2, 128, 128), F32),
        dma((2, 4)), dma((4, 4)), dma((8, 4)),
        dma((9, 3)), dma((9, 3)), dma((9, 7)), dma((9, 7)),
        dma((9, 8)), dma((9, 8)), dma((9, 3)), dma((9, 3)), dma, dma,
    ]
    return pl.pallas_call(
        functools.partial(kernel, comm),
        in_specs=[hbm] * 4 + [vmem],
        out_specs=(hbm, vmem),
        out_shape=(
            jax.ShapeDtypeStruct((16, 2, 128, 128), F32),
            jax.ShapeDtypeStruct((2, 128, 128), F32),
        ),
        scratch_shapes=scratch,
        compiler_params=pltpu.CompilerParams(
            vmem_limit_bytes=56 * 2**20,
            **(dict(collective_id=0, has_side_effects=True) if comm else {}),
        ),
        name="overturning",
    )(v, h, k, w, width)


def shards(velocity, thickness, class_index, layer_weight, zonal_width):
    pad, total = overturning(velocity, thickness, class_index, layer_weight, zonal_width.reshape(2, -1) * (1 / 64.0))
    hbm = pl.BlockSpec(memory_space=pl.ANY)
    vmem = pl.BlockSpec(memory_space=pltpu.VMEM)
    psi, mean, var = pl.pallas_call(
        finals,
        in_specs=[hbm, vmem],
        out_specs=(hbm, vmem, vmem),
        out_shape=(
            jax.ShapeDtypeStruct((16, C // 2, 256), F32),
            jax.ShapeDtypeStruct((4, C // 2), F32),
            jax.ShapeDtypeStruct((4, C // 2), F32),
        ),
        scratch_shapes=[pltpu.SemaphoreType.DMA((16, 2))],
        compiler_params=pltpu.CompilerParams(vmem_limit_bytes=60 * 2**20),
        name="finals",
    )(pad, total)
    return psi, mean.T, var.T


def solution(mesh):
    cells = P("tm", "lon", None, None)
    in_specs = (cells, cells, cells, cells, P())
    out_specs = (P("tm", "cls", None), P("cls", ("tm", "lon")), P("cls", ("tm", "lon")))
    return jax.shard_map(shards, mesh=mesh, in_specs=in_specs, out_specs=out_specs, check_vma=False)
```

```python
import functools
import jax
import jax.numpy as jnp
from jax import lax
from jax.experimental import pallas as pl
from jax.experimental.pallas import tpu as pltpu
from jax.sharding import PartitionSpec as P

C = 240
GROUPS = 8
LAST = 8
NT = (((1,), (1,)), ((), ()))
MESH = pl.DeviceIdType.MESH
F32, BF16 = jnp.float32, jnp.bfloat16


def prepare(raw, turned, chunk):
    lons = pl.ds(chunk * 8, 8)
    cells = pl.ds(pl.multiple_of(chunk * 256, 256), 256)
    speed, layer, lighter, share = (ref[lons].reshape(256, 256) for ref in raw)
    v_t, h_t, hi_t, lo_t, q_t, e_t = turned
    v_t[:, cells] = speed.T
    h_t[:, cells] = (layer * 64.0).T
    k = lighter.astype(F32)
    hi = (k * (1 / 15.0) + (129 - 7 / 15.0)).astype(BF16)
    hi_t[:, cells] = hi.T
    lo_t[:, cells] = (k.astype(BF16) - (hi - 129.0) * 15.0).T
    part = layer.astype(F32) * share.astype(F32)
    q = part.astype(BF16)
    q_t[:, cells] = q.T
    e_t[:, cells] = (part - q.astype(F32)).astype(BF16).T


def group_sums(turned, rows, diagonal):
    total = None
    for start in range(0, 1024, 256):
        cells = slice(start, start + 256)
        v, h, hi, lo, q, e = (ref[rows, cells] for ref in turned)
        zero = jnp.zeros_like(v)
        a = jnp.concatenate([jnp.where(hi == float(x + 129), v, zero) for x in range(16)], axis=0)
        b, f = [], []
        below = zero
        for x in range(15):
            here = lo == float(x)
            b.append(jnp.where(here, q, below))
            f.append(jnp.where(here, e, zero))
            below = jnp.where(here, h, below)
        b = jnp.concatenate(b + [below], axis=0)
        f = jnp.concatenate(f + [zero], axis=0)
        part = lax.dot_general(
            jnp.concatenate([b, f], axis=0), a, NT, preferred_element_type=F32
        )
        total = part if total is None else total + part
    total = total[:256] + total[256:]
    return jnp.where(diagonal[None], total.reshape(16, 16, 256), 0.0).sum(1)


def arrange(sums, width, units, slot_of):
    lane = lax.broadcasted_iota(jnp.int32, (16, 128), 1)
    offset = jnp.zeros((1, 128), F32)
    for part in range(2):
        x = [sums[g, :, part * 128 : part * 128 + 128] for g in range(8)]
        for d in (4, 2, 1):
            high = (lane & (16 * d)) != 0
            y = list(x)
            for i in range(8):
                if i & d == 0:
                    y[i] = jnp.where(high, pltpu.roll(x[i + d], 16 * d, 1), x[i])
                    y[i + d] = jnp.where(high, x[i + d], pltpu.roll(x[i], 128 - 16 * d, 1))
            x = y
        for i in range(8):
            units[slot_of(part), 15 * i : 15 * i + 16, :] = (x[i] + offset) * width
            offset = offset + x[i][15:16]


def kernel(comm, v_hbm, h_hbm, k_hbm, w_hbm, width, psi_hbm, total_ref, *scratch):
    (raw_v, raw_h, raw_k, raw_w), scratch = scratch[:4], scratch[4:]
    even, odd, scratch = scratch[:6], scratch[6:12], scratch[12:]
    (sums, send, got_1, mid, got_2, own, pad, stat, got_3, read_sem, quarter_sem, write_sem) = scratch[:12]
    (s1, r1, s2, r2, s3, r3, s4, r4, s5, r5) = scratch[12:]
    if comm:
        tm, lon, cls = lax.axis_index("tm"), lax.axis_index("lon"), lax.axis_index("cls")
    else:
        tm, lon, cls = jnp.int32(0), jnp.int32(0), jnp.int32(0)
    zz, xx, yy = lon // 8, (lon // 2) % 4, lon % 2
    n_own = 8

    def read(s, slot):
        return [
            pltpu.make_async_copy(src.at[cls * n_own + s], dst.at[slot], read_sem.at[slot, i])
            for i, (src, dst) in enumerate(
                zip((v_hbm, h_hbm, k_hbm, w_hbm), (raw_v, raw_h, raw_k, raw_w))
            )
        ]

    spots = ((xx, zz), (zz, xx))
    cols, col_lon, place, place_lon = [], [], [], []
    for p, (a, b) in enumerate(spots):
        step_a, step_b = (8, 2) if p else (2, 8)
        near = [a] + [(a + rel) % 4 for rel in (1, 2, 3)]
        cols.append(near)
        col_lon.append([c * step_a + b * step_b + yy for c in near])
        me = b * 2 + yy
        near = [me] + [(me + rel) % 8 for rel in range(1, 8)]
        place.append(near)
        place_lon.append([a * step_a + (n // 2) * step_b + n % 2 for n in near])
    home = [(cls + a // 2) % 2 for a, _ in spots]

    def size(job):
        return 128 if job[3] is None else 64

    def unit_of(job, col):
        half = job[3]
        return col, 0 if half is None else half * 64, col % 2

    def base(job, n):
        return 0 if job[3] is None else job[3] * n

    def span(start, n):
        return pl.ds(start if isinstance(start, int) else pl.multiple_of(start, 8), n)

    def first(job, rel):
        i, p, s, _ = job
        n = size(job)
        u, r, _ = unit_of(job, cols[p][rel])
        return pltpu.make_async_remote_copy(
            src_ref=send.at[s, u, span(r, n)], dst_ref=got_1.at[s, 3 - rel, span(base(job, 64), n)],
            send_sem=s1.at[i, rel - 1], recv_sem=r1.at[i, 3 - rel],
            device_id={"lon": col_lon[p][rel]}, device_id_type=MESH)

    def second(job, rel):
        i, p, s, _ = job
        n = size(job) // 8
        return pltpu.make_async_remote_copy(
            src_ref=mid.at[s, span(base(job, 64) + place[p][rel] * n, n)],
            dst_ref=got_2.at[s, 7 - rel, span(base(job, 8), n)],
            send_sem=s2.at[i, rel - 1], recv_sem=r2.at[i, 7 - rel],
            device_id={"lon": place_lon[p][rel]}, device_id_type=MESH)

    def target(job, group, rel):
        _, p, s, _ = job
        n = size(job) // 8
        _, r, half = unit_of(job, cols[p][0])
        return pad.at[group * n_own + s, half, span(r + place[p][rel] * n, n)]

    def third(job, rel):
        i, p, s, _ = job
        return pltpu.make_async_remote_copy(
            src_ref=own.at[s, span(base(job, 8), size(job) // 8)], dst_ref=target(job, cls, 0),
            send_sem=s3.at[i, rel], recv_sem=r3.at[i, (8 - rel) % 8],
            device_id={"lon": place_lon[p][rel], "cls": home[p]}, device_id_type=MESH)

    def third_got(job, rel):
        i, p, s, _ = job
        return pltpu.make_async_remote_copy(
            src_ref=own.at[s, span(base(job, 8), size(job) // 8)], dst_ref=target(job, home[p], rel),
            send_sem=s3.at[i, rel], recv_sem=r3.at[i, rel],
            device_id={"lon": place_lon[p][rel], "cls": home[p]}, device_id_type=MESH)

    def spread(job, rel):
        _, p, s, _ = job
        col = cols[p][rel]
        _, r, half = unit_of(job, col)
        return pad.at[(cls + col // 2) % 2 * n_own + s, half, span(r, size(job))]

    def fourth(job, rel):
        i, p, _, _ = job
        return pltpu.make_async_remote_copy(
            src_ref=spread(job, 0), dst_ref=spread(job, 0), send_sem=s4.at[i, rel - 1],
            recv_sem=r4.at[i, 3 - rel], device_id={"lon": col_lon[p][rel]}, device_id_type=MESH)

    def fourth_got(job, rel):
        i, p, _, _ = job
        dst = spread(job, rel)
        return pltpu.make_async_remote_copy(
            src_ref=dst, dst_ref=dst, send_sem=s4.at[i, rel - 1], recv_sem=r4.at[i, rel - 1],
            device_id={"lon": col_lon[p][rel]}, device_id_type=MESH)

    def write(s):
        return [
            pltpu.make_async_copy(
                pad.at[base + s, half],
                psi_hbm.at[base + s, half],
                write_sem.at[s, base // 4 + half])
            for base in (0, n_own) for half in (0, 1)
        ]

    def start_1(job):
        for rel in (1, 2, 3):
            first(job, rel).start()

    def start_2(job):
        _, p, s, _ = job
        n = size(job)
        u, r, _ = unit_of(job, cols[p][0])
        rows = span(base(job, 64), n)
        for rel in (1, 2, 3):
            first(job, rel).wait_recv()
        mid[s, rows] = send[s, u, span(r, n)] + got_1[s, 0, rows] + got_1[s, 1, rows] + got_1[s, 2, rows]
        for rel in range(1, 8):
            second(job, rel).start()

    def start_3(job):
        _, p, s, _ = job
        n = size(job) // 8
        rows = span(base(job, 8), n)
        for rel in range(1, 8):
            second(job, rel).wait_recv()
        total = mid[s, span(base(job, 64) + place[p][0] * n, n)]
        for i in range(7):
            total = total + got_2[s, i, rows]
        own[s, rows] = total

        @pl.when(cols[p][0] < 2)
        def _():
            target(job, cls, 0)[...] = total

        @pl.when(cols[p][0] >= 2)
        def _():
            third(job, 0).start()

        for rel in range(1, 8):
            third(job, rel).start()

    def start_4(job):
        p = job[1]

        @pl.when(cols[p][0] >= 2)
        def _():
            third_got(job, 0).wait_recv()

        for rel in range(1, 8):
            third_got(job, rel).wait_recv()
        for rel in (1, 2, 3):
            fourth(job, rel).start()

    def take(s):
        for half in range(2):
            one, two = stat[half, 0], stat[half, 1]
            for base in (0, n_own):
                x = pad[base + s, half]
                one = one + x
                two = two + x * x
            stat[half, 0] = one
            stat[half, 1] = two

    def finish(job):
        for rel in (1, 2, 3):
            fourth_got(job, rel).wait_recv()
        if job[0] is not LAST - 1:
            for copy in write(job[2]):
                copy.start()
            take(job[2])

    def drain(job):
        for rel in (1, 2, 3):
            first(job, rel).wait_send()
            fourth(job, rel).wait_send()
        for rel in range(1, 8):
            second(job, rel).wait_send()
            third(job, rel).wait_send()

        @pl.when(cols[job[1]][0] >= 2)
        def _():
            third(job, 0).wait_send()

        if job[0] is not LAST - 1:
            for copy in write(job[2]):
                copy.wait()

    def whole(q, s):
        return (s, q, s, None)

    ends = ((LAST - 1, 1, 7, 0), (LAST, 0, 7, 1))

    barrier = None
    if comm:
        barrier = pltpu.get_barrier_semaphore()
        def greet(to, where):
            pl.semaphore_signal(barrier, inc=1, device_id=where, device_id_type=MESH)

        for y in range(2):
            for i in range(4):
                for near in range(2):
                    group = (cls + near) % 2
                    row = {"lon": ((zz + i) % 4) * 8 + xx * 2 + (yy + y) % 2, "cls": group}
                    if near or i or y:
                        greet(None, row)
                    if i:
                        greet(None, {"lon": zz * 8 + ((xx + i) % 4) * 2 + (yy + y) % 2, "cls": group})
        greet(None, {"tm": 1 - tm})
    n_greet = 2 * 2 * 4 - 1 + 2 * 2 * 3 + 1

    lane = lax.broadcasted_iota(jnp.int32, (16, 256), 1)
    row = lax.broadcasted_iota(jnp.int32, (16, 256), 0)
    diagonal = (lane & 15) == row
    raws = [[ref.at[slot] for ref in (raw_v, raw_h, raw_k, raw_w)] for slot in range(2)]

    def quarter(chunk):
        lons = pl.ds(chunk * 8, 8)
        return [
            pltpu.make_async_copy(src.at[cls * n_own, lons], dst.at[0, lons], quarter_sem.at[chunk, i])
            for i, (src, dst) in enumerate(
                zip((v_hbm, h_hbm, k_hbm, w_hbm), (raw_v, raw_h, raw_k, raw_w))
            )
        ]

    for chunk in range(4):
        for copy in quarter(chunk):
            copy.start()
    for copy in read(1, 1):
        copy.start()
    stat[...] = jnp.zeros_like(stat)
    def pad_rows(s, carry):
        for u in range(4):
            send[s, u, pl.ds(C // 2, 8), :] = jnp.zeros((8, 128), F32)
        return carry

    lax.fori_loop(0, n_own, pad_rows, 0)

    def prologue(chunk, carry):
        for copy in quarter(chunk):
            copy.wait()
        prepare(raws[0], even, chunk)
        return carry

    lax.fori_loop(0, 4, prologue, 0)

    def compute(s, p):
        here, there = (odd, even) if p else (even, odd)

        @pl.when(s + 2 < n_own)
        def _():
            for copy in read(s + 2, p):
                copy.start()

        @pl.when(s + 1 < n_own)
        def _():
            for copy in read(s + 1, 1 - p):
                copy.wait()

        def step(j, carry):
            for c in range(GROUPS // 4):
                prepare(raws[1 - p], there, j * (GROUPS // 4) + c)
            for g in range(GROUPS):
                rows = pl.ds(pl.multiple_of((j * GROUPS + g) * 16, 16), 16)
                sums[j * GROUPS + g] = group_sums(here, rows, diagonal)
            return carry

        lax.fori_loop(0, 16 // GROUPS, step, 0)
        for j in range(2):
            arrange(sums.at[pl.ds(j * 8, 8)], width[j : j + 1, :] * (1 / 64.0), send.at[s], lambda cut: ((cls + cut) % 2) * 2 + j)

    def pair(t, carry):
        for p in range(2):
            s = 2 * t + p
            compute(s, p)
            if not comm:
                continue

            def advance():
                start_1(whole(p, s))
                for least, go, q in ((1, start_2, 1 - p), (2, start_3, p), (3, start_4, 1 - p), (4, finish, p)):
                    if least <= p:
                        go(whole(q, s - least))
                    else:
                        @pl.when(s >= least)
                        def _(go=go, q=q, least=least):
                            go(whole(q, s - least))

            if p == 0:
                @pl.when(t == 0)
                def _():
                    pl.semaphore_wait(barrier, n_greet)
                advance()
            else:
                pl.when(s < n_own - 1)(advance)
        return carry

    lax.fori_loop(0, n_own // 2, pair, 0)
    if comm:
        for job in ends:
            start_1(job)
        start_2(whole(0, 6))
        start_3(whole(1, 5))
        start_4(whole(0, 4))
        finish(whole(1, 3))
        for job in ends:
            start_2(job)
        start_3(whole(0, 6))
        start_4(whole(1, 5))
        finish(whole(0, 4))
        for job in ends:
            start_3(job)
        start_4(whole(0, 6))
        finish(whole(1, 5))
        for job in ends:
            start_4(job)
        finish(whole(0, 6))
        for job in ends:
            finish(job)
        swap = pltpu.make_async_remote_copy(
            src_ref=stat.at[1 - tm], dst_ref=got_3, send_sem=s5, recv_sem=r5,
            device_id={"tm": 1 - tm}, device_id_type=MESH)
        swap.start()

        def drains(t, carry):
            drain(whole(0, 2 * t))
            drain(whole(1, 2 * t + 1))
            return carry

        lax.fori_loop(0, n_own // 2 - 1, drains, 0)
        drain(whole(0, 6))
        for job in ends:
            drain(job)
        swap.wait()
    else:
        for s in range(8):
            pad[s, 0] = send[s, 0]
            pad[s, 1] = send[s, 1]
            pad[s + 8, 0] = send[s, 2]
            pad[s + 8, 1] = send[s, 3]
        for s in (0, 7):
            for copy in write(s):
                copy.start()
            for copy in write(s):
                copy.wait()
        got_3[...] = jnp.zeros_like(got_3)
    total_ref[...] = stat[tm] + got_3[...]


def finals(pad_hbm, total, psi_hbm, mean_ref, var_ref, pad, read_sem, sem):
    reads = [
        pltpu.make_async_copy(pad_hbm.at[pl.ds(4 * i, 4)], pad.at[pl.ds(4 * i, 4)], read_sem.at[i])
        for i in range(4)
    ]
    writes = [
        pltpu.make_async_copy(
            pad.at[s, half, pl.ds(0, C // 2)], psi_hbm.at[s, :, pl.ds(half * 128, 128)], sem.at[s, half]
        )
        for s in range(16)
        for half in range(2)
    ]
    for copy in reads:
        copy.start()
    mean = total[0] / 32.0
    var = total[1] / 32.0 - mean * mean
    shift = (128 - lax.axis_index("lon") * 4) % 128
    mean_ref[...] = pltpu.roll(mean, shift, 1).T[:4, : C // 2]
    var_ref[...] = pltpu.roll(var, shift, 1).T[:4, : C // 2]
    for i in range(4):
        reads[i].wait()
        for copy in writes[8 * i : 8 * i + 8]:
            copy.start()
    for copy in writes:
        copy.wait()


def overturning(v, h, k, w, width, comm=True):
    dma = pltpu.SemaphoreType.DMA
    hbm = pl.BlockSpec(memory_space=pl.ANY)
    vmem = pl.BlockSpec(memory_space=pltpu.VMEM)
    scratch = [pltpu.VMEM((2, 32, 32, 256), d) for d in (BF16, BF16, jnp.int32, jnp.int32)]
    scratch += [pltpu.VMEM((256, 1024), BF16)] * 12
    scratch += [
        pltpu.VMEM((16, 16, 256), F32),
        pltpu.VMEM((8, 4, 128, 128), F32),
        pltpu.VMEM((8, 3, 128, 128), F32),
        pltpu.VMEM((8, 128, 128), F32),
        pltpu.VMEM((8, 7, 16, 128), F32),
        pltpu.VMEM((8, 16, 128), F32),
        pltpu.VMEM((16, 2, 128, 128), F32),
        pltpu.VMEM((2, 2, 128, 128), F32),
        pltpu.VMEM((2, 128, 128), F32),
        dma((2, 4)), dma((4, 4)), dma((8, 4)),
        dma((9, 3)), dma((9, 3)), dma((9, 7)), dma((9, 7)),
        dma((9, 8)), dma((9, 8)), dma((9, 3)), dma((9, 3)), dma, dma,
    ]
    return pl.pallas_call(
        functools.partial(kernel, comm),
        in_specs=[hbm] * 4 + [vmem],
        out_specs=(hbm, vmem),
        out_shape=(
            jax.ShapeDtypeStruct((16, 2, 128, 128), F32),
            jax.ShapeDtypeStruct((2, 128, 128), F32),
        ),
        scratch_shapes=scratch,
        compiler_params=pltpu.CompilerParams(
            vmem_limit_bytes=56 * 2**20,
            **(dict(collective_id=0, has_side_effects=True) if comm else {}),
        ),
        name="overturning",
    )(v, h, k, w, width)


def shards(velocity, thickness, class_index, layer_weight, zonal_width):
    pad, total = overturning(velocity, thickness, class_index, layer_weight, zonal_width.reshape(2, -1))
    hbm = pl.BlockSpec(memory_space=pl.ANY)
    vmem = pl.BlockSpec(memory_space=pltpu.VMEM)
    psi, mean, var = pl.pallas_call(
        finals,
        in_specs=[hbm, vmem],
        out_specs=(hbm, vmem, vmem),
        out_shape=(
            jax.ShapeDtypeStruct((16, C // 2, 256), F32),
            jax.ShapeDtypeStruct((4, C // 2), F32),
            jax.ShapeDtypeStruct((4, C // 2), F32),
        ),
        scratch_shapes=[
            pltpu.VMEM((16, 2, 128, 128), F32),
            pltpu.SemaphoreType.DMA((4,)),
            pltpu.SemaphoreType.DMA((16, 2)),
        ],
        compiler_params=pltpu.CompilerParams(vmem_limit_bytes=60 * 2**20),
        name="finals",
    )(pad, total)
    return psi, mean.T, var.T


def solution(mesh):
    cells = P("tm", "lon", None, None)
    in_specs = (cells, cells, cells, cells, P())
    out_specs = (P("tm", "cls", None), P("cls", ("tm", "lon")), P("cls", ("tm", "lon")))
    return jax.shard_map(shards, mesh=mesh, in_specs=in_specs, out_specs=out_specs, check_vma=False)
```

```python
import functools
import jax
import jax.numpy as jnp
from jax import lax
from jax.experimental import pallas as pl
from jax.experimental.pallas import tpu as pltpu
from jax.sharding import PartitionSpec as P

C = 240
GROUPS = 8
LAST = 8
NT = (((1,), (1,)), ((), ()))
MESH = pl.DeviceIdType.MESH
F32, BF16 = jnp.float32, jnp.bfloat16


def prepare(raw, turned, chunk):
    lons = pl.ds(chunk * 8, 8)
    cells = pl.ds(pl.multiple_of(chunk * 256, 256), 256)
    for src, dst in zip(raw, turned):
        dst[:, cells] = src[lons].reshape(256, 256).astype(BF16).T


def group_sums(turned, rows):
    total = None
    for start in range(0, 1024, 256):
        cells = slice(start, start + 256)
        v, thick, k, w = (ref[rows, cells] for ref in turned)
        hi = (k.astype(F32) * (1 / 15.0) + (129 - 7 / 15.0)).astype(BF16)
        lo = k - (hi - 129.0) * 15.0
        share = thick.astype(F32) * w.astype(F32)
        q = share.astype(BF16)
        e = (share - q.astype(F32)).astype(BF16)
        h = thick * 64.0
        zero = jnp.zeros_like(v)
        a = jnp.concatenate([jnp.where(hi == float(x + 129), v, zero) for x in range(16)], axis=0)
        b, f = [], []
        below = zero
        for x in range(15):
            here = lo == float(x)
            b.append(jnp.where(here, q, below))
            f.append(jnp.where(here, e, zero))
            below = jnp.where(here, h, below)
        b = jnp.concatenate(b + [below], axis=0)
        f = jnp.concatenate(f + [zero], axis=0)
        part = lax.dot_general(
            jnp.concatenate([b, f], axis=0), a, NT, preferred_element_type=F32
        )
        total = part if total is None else total + part
    total = total[:256] + total[256:]
    return pick(total)


def pick(total):
    lane = lax.broadcasted_iota(jnp.int32, (8, 128), 1)
    sub = lax.broadcasted_iota(jnp.int32, (8, 128), 0)
    blocks = []
    for start in (0, 128):
        cols = slice(start, start + 128)
        upper = (lane & 8) != 0
        x = [
            jnp.where(upper, total[16 * i + 8 : 16 * i + 16, cols], total[16 * i : 16 * i + 8, cols])
            for i in range(16)
        ]
        for d in (4, 2, 1):
            moved = (lane & d) != 0
            stays = (lane & d) == (sub & d)
            y = []
            for i in range(0, len(x), 2 * d):
                for one, two in zip(x[i : i + d], x[i + d : i + 2 * d]):
                    keep = jnp.where(moved, two, one)
                    if d == 4:
                        move = pltpu.roll(jnp.where(moved, one, two), 4, 0)
                    else:
                        move = jnp.where(moved, pltpu.roll(one, 8 - d, 0), pltpu.roll(two, d, 0))
                    y.append(jnp.where(stays, keep, move))
            x = y
        blocks.append(jnp.concatenate(x, axis=0))
    return jnp.concatenate(blocks, axis=1)


def arrange(sums, width, units, slot_of):
    lane = lax.broadcasted_iota(jnp.int32, (16, 128), 1)
    offset = jnp.zeros((1, 128), F32)
    for part in range(2):
        x = [sums[g, :, part * 128 : part * 128 + 128] for g in range(8)]
        for d in (4, 2, 1):
            high = (lane & (16 * d)) != 0
            y = list(x)
            for i in range(8):
                if i & d == 0:
                    y[i] = jnp.where(high, pltpu.roll(x[i + d], 16 * d, 1), x[i])
                    y[i + d] = jnp.where(high, x[i + d], pltpu.roll(x[i], 128 - 16 * d, 1))
            x = y
        for i in range(8):
            units[slot_of(part), 15 * i : 15 * i + 16, :] = (x[i] + offset) * width
            offset = offset + x[i][15:16]


def kernel(comm, v_hbm, h_hbm, k_hbm, w_hbm, width, psi_hbm, total_ref, *scratch):
    (raw_v, raw_h, raw_k, raw_w), scratch = scratch[:4], scratch[4:]
    even, odd, scratch = scratch[:4], scratch[4:8], scratch[8:]
    (sums, send, got_1, mid, got_2, own, pad, stat, got_3, read_sem, quarter_sem, write_sem) = scratch[:12]
    (s1, r1, s2, r2, s3, r3, s4, r4, s5, r5) = scratch[12:]
    if comm:
        tm, lon, cls = lax.axis_index("tm"), lax.axis_index("lon"), lax.axis_index("cls")
    else:
        tm, lon, cls = jnp.int32(0), jnp.int32(0), jnp.int32(0)
    zz, xx, yy = lon // 8, (lon // 2) % 4, lon % 2
    n_own = 8

    def read(s, slot):
        return [
            pltpu.make_async_copy(src.at[cls * n_own + s], dst.at[slot], read_sem.at[slot, i])
            for i, (src, dst) in enumerate(
                zip((v_hbm, h_hbm, k_hbm, w_hbm), (raw_v, raw_h, raw_k, raw_w))
            )
        ]

    spots = ((xx, zz), (zz, xx))
    cols, col_lon, place, place_lon = [], [], [], []
    for p, (a, b) in enumerate(spots):
        step_a, step_b = (8, 2) if p else (2, 8)
        near = [a] + [(a + rel) % 4 for rel in (1, 2, 3)]
        cols.append(near)
        col_lon.append([c * step_a + b * step_b + yy for c in near])
        me = b * 2 + yy
        near = [me] + [(me + rel) % 8 for rel in range(1, 8)]
        place.append(near)
        place_lon.append([a * step_a + (n // 2) * step_b + n % 2 for n in near])
    home = [(cls + a // 2) % 2 for a, _ in spots]

    def size(job):
        return 128 if job[3] is None else 64

    def unit_of(job, col):
        half = job[3]
        return col, 0 if half is None else half * 64, col % 2

    def base(job, n):
        return 0 if job[3] is None else job[3] * n

    def span(start, n):
        return pl.ds(start if isinstance(start, int) else pl.multiple_of(start, 8), n)

    def first(job, rel):
        i, p, s, _ = job
        n = size(job)
        u, r, _ = unit_of(job, cols[p][rel])
        return pltpu.make_async_remote_copy(
            src_ref=send.at[s, u, span(r, n)], dst_ref=got_1.at[s, 3 - rel, span(base(job, 64), n)],
            send_sem=s1.at[i, rel - 1], recv_sem=r1.at[i, 3 - rel],
            device_id={"lon": col_lon[p][rel]}, device_id_type=MESH)

    def second(job, rel):
        i, p, s, _ = job
        n = size(job) // 8
        return pltpu.make_async_remote_copy(
            src_ref=mid.at[s, span(base(job, 64) + place[p][rel] * n, n)],
            dst_ref=got_2.at[s, 7 - rel, span(base(job, 8), n)],
            send_sem=s2.at[i, rel - 1], recv_sem=r2.at[i, 7 - rel],
            device_id={"lon": place_lon[p][rel]}, device_id_type=MESH)

    def target(job, group, rel):
        _, p, s, _ = job
        n = size(job) // 8
        _, r, half = unit_of(job, cols[p][0])
        return pad.at[group * n_own + s, half, span(r + place[p][rel] * n, n)]

    def third(job, rel):
        i, p, s, _ = job
        return pltpu.make_async_remote_copy(
            src_ref=own.at[s, span(base(job, 8), size(job) // 8)], dst_ref=target(job, cls, 0),
            send_sem=s3.at[i, rel], recv_sem=r3.at[i, (8 - rel) % 8],
            device_id={"lon": place_lon[p][rel], "cls": home[p]}, device_id_type=MESH)

    def third_got(job, rel):
        i, p, s, _ = job
        return pltpu.make_async_remote_copy(
            src_ref=own.at[s, span(base(job, 8), size(job) // 8)], dst_ref=target(job, home[p], rel),
            send_sem=s3.at[i, rel], recv_sem=r3.at[i, rel],
            device_id={"lon": place_lon[p][rel], "cls": home[p]}, device_id_type=MESH)

    def spread(job, rel):
        _, p, s, _ = job
        col = cols[p][rel]
        _, r, half = unit_of(job, col)
        return pad.at[(cls + col // 2) % 2 * n_own + s, half, span(r, size(job))]

    def fourth(job, rel):
        i, p, _, _ = job
        return pltpu.make_async_remote_copy(
            src_ref=spread(job, 0), dst_ref=spread(job, 0), send_sem=s4.at[i, rel - 1],
            recv_sem=r4.at[i, 3 - rel], device_id={"lon": col_lon[p][rel]}, device_id_type=MESH)

    def fourth_got(job, rel):
        i, p, _, _ = job
        dst = spread(job, rel)
        return pltpu.make_async_remote_copy(
            src_ref=dst, dst_ref=dst, send_sem=s4.at[i, rel - 1], recv_sem=r4.at[i, rel - 1],
            device_id={"lon": col_lon[p][rel]}, device_id_type=MESH)

    def write(s):
        return [
            pltpu.make_async_copy(
                pad.at[base + s, half],
                psi_hbm.at[base + s, half],
                write_sem.at[s, base // 4 + half])
            for base in (0, n_own) for half in (0, 1)
        ]

    def start_1(job):
        for rel in (1, 2, 3):
            first(job, rel).start()

    def start_2(job):
        _, p, s, _ = job
        n = size(job)
        u, r, _ = unit_of(job, cols[p][0])
        rows = span(base(job, 64), n)
        for rel in (1, 2, 3):
            first(job, rel).wait_recv()
        mid[s, rows] = send[s, u, span(r, n)] + got_1[s, 0, rows] + got_1[s, 1, rows] + got_1[s, 2, rows]
        for rel in range(1, 8):
            second(job, rel).start()

    def start_3(job):
        _, p, s, _ = job
        n = size(job) // 8
        rows = span(base(job, 8), n)
        for rel in range(1, 8):
            second(job, rel).wait_recv()
        total = mid[s, span(base(job, 64) + place[p][0] * n, n)]
        for i in range(7):
            total = total + got_2[s, i, rows]
        own[s, rows] = total

        @pl.when(cols[p][0] < 2)
        def _():
            target(job, cls, 0)[...] = total

        @pl.when(cols[p][0] >= 2)
        def _():
            third(job, 0).start()

        for rel in range(1, 8):
            third(job, rel).start()

    def start_4(job):
        p = job[1]

        @pl.when(cols[p][0] >= 2)
        def _():
            third_got(job, 0).wait_recv()

        for rel in range(1, 8):
            third_got(job, rel).wait_recv()
        for rel in (1, 2, 3):
            fourth(job, rel).start()

    def take(s):
        for half in range(2):
            one, two = stat[half, 0], stat[half, 1]
            for base in (0, n_own):
                x = pad[base + s, half]
                one = one + x
                two = two + x * x
            stat[half, 0] = one
            stat[half, 1] = two

    def finish(job):
        for rel in (1, 2, 3):
            fourth_got(job, rel).wait_recv()
        if job[0] is not LAST - 1:
            for copy in write(job[2]):
                copy.start()
            take(job[2])

    def drain(job):
        for rel in (1, 2, 3):
            first(job, rel).wait_send()
            fourth(job, rel).wait_send()
        for rel in range(1, 8):
            second(job, rel).wait_send()
            third(job, rel).wait_send()

        @pl.when(cols[job[1]][0] >= 2)
        def _():
            third(job, 0).wait_send()

        if job[0] is not LAST - 1:
            for copy in write(job[2]):
                copy.wait()

    def whole(q, s):
        return (s, q, s, None)

    ends = ((LAST - 1, 1, 7, 0), (LAST, 0, 7, 1))

    barrier = None
    if comm:
        barrier = pltpu.get_barrier_semaphore()
        def greet(to, where):
            pl.semaphore_signal(barrier, inc=1, device_id=where, device_id_type=MESH)

        for y in range(2):
            for i in range(4):
                for near in range(2):
                    group = (cls + near) % 2
                    row = {"lon": ((zz + i) % 4) * 8 + xx * 2 + (yy + y) % 2, "cls": group}
                    if near or i or y:
                        greet(None, row)
                    if i:
                        greet(None, {"lon": zz * 8 + ((xx + i) % 4) * 2 + (yy + y) % 2, "cls": group})
        greet(None, {"tm": 1 - tm})
    n_greet = 2 * 2 * 4 - 1 + 2 * 2 * 3 + 1

    raws = [[ref.at[slot] for ref in (raw_v, raw_h, raw_k, raw_w)] for slot in range(2)]

    def quarter(chunk):
        lons = pl.ds(chunk * 8, 8)
        return [
            pltpu.make_async_copy(src.at[cls * n_own, lons], dst.at[0, lons], quarter_sem.at[chunk, i])
            for i, (src, dst) in enumerate(
                zip((v_hbm, h_hbm, k_hbm, w_hbm), (raw_v, raw_h, raw_k, raw_w))
            )
        ]

    for chunk in range(4):
        for copy in quarter(chunk):
            copy.start()
    for copy in read(1, 1):
        copy.start()
    stat[...] = jnp.zeros_like(stat)
    def pad_rows(s, carry):
        for u in range(4):
            send[s, u, pl.ds(C // 2, 8), :] = jnp.zeros((8, 128), F32)
        return carry

    lax.fori_loop(0, n_own, pad_rows, 0)

    def prologue(chunk, carry):
        for copy in quarter(chunk):
            copy.wait()
        prepare(raws[0], even, chunk)
        return carry

    lax.fori_loop(0, 4, prologue, 0)

    def compute(s, p):
        here, there = (odd, even) if p else (even, odd)

        @pl.when(s + 2 < n_own)
        def _():
            for copy in read(s + 2, p):
                copy.start()

        @pl.when(s + 1 < n_own)
        def _():
            for copy in read(s + 1, 1 - p):
                copy.wait()

        def run(more):
            def step(j, carry):
                for c in range(GROUPS // 4 if more else 0):
                    prepare(raws[1 - p], there, j * (GROUPS // 4) + c)
                for g in range(GROUPS):
                    rows = pl.ds(pl.multiple_of((j * GROUPS + g) * 16, 16), 16)
                    sums[j * GROUPS + g] = group_sums(here, rows)
                return carry

            lax.fori_loop(0, 16 // GROUPS, step, 0)

        if p == 0:
            run(True)
        else:
            pl.when(s < n_own - 1)(lambda: run(True))
            pl.when(s == n_own - 1)(lambda: run(False))
        for j in range(2):
            arrange(sums.at[pl.ds(j * 8, 8)], width[j : j + 1, :] * (1 / 64.0), send.at[s], lambda cut: ((cls + cut) % 2) * 2 + j)

    def pair(t, carry):
        for p in range(2):
            s = 2 * t + p
            compute(s, p)
            if not comm:
                continue

            def advance():
                start_1(whole(p, s))
                for least, go, q in ((1, start_2, 1 - p), (2, start_3, p), (3, start_4, 1 - p), (4, finish, p)):
                    if least <= p:
                        go(whole(q, s - least))
                    else:
                        @pl.when(s >= least)
                        def _(go=go, q=q, least=least):
                            go(whole(q, s - least))

            if p == 0:
                @pl.when(t == 0)
                def _():
                    pl.semaphore_wait(barrier, n_greet)
                advance()
            else:
                pl.when(s < n_own - 1)(advance)
        return carry

    lax.fori_loop(0, n_own // 2, pair, 0)
    if comm:
        for job in ends:
            start_1(job)
        start_2(whole(0, 6))
        start_3(whole(1, 5))
        start_4(whole(0, 4))
        finish(whole(1, 3))
        for job in ends:
            start_2(job)
        start_3(whole(0, 6))
        start_4(whole(1, 5))
        finish(whole(0, 4))
        for job in ends:
            start_3(job)
        start_4(whole(0, 6))
        finish(whole(1, 5))
        for job in ends:
            start_4(job)
        finish(whole(0, 6))
        for job in ends:
            finish(job)
        swap = pltpu.make_async_remote_copy(
            src_ref=stat.at[1 - tm], dst_ref=got_3, send_sem=s5, recv_sem=r5,
            device_id={"tm": 1 - tm}, device_id_type=MESH)
        swap.start()

        def drains(t, carry):
            drain(whole(0, 2 * t))
            drain(whole(1, 2 * t + 1))
            return carry

        lax.fori_loop(0, n_own // 2 - 1, drains, 0)
        drain(whole(0, 6))
        for job in ends:
            drain(job)
        swap.wait()
    else:
        for s in range(8):
            pad[s, 0] = send[s, 0]
            pad[s, 1] = send[s, 1]
            pad[s + 8, 0] = send[s, 2]
            pad[s + 8, 1] = send[s, 3]
        for s in (0, 7):
            for copy in write(s):
                copy.start()
            for copy in write(s):
                copy.wait()
        got_3[...] = jnp.zeros_like(got_3)
    total_ref[...] = stat[tm] + got_3[...]


def finals(pad_hbm, total, psi_hbm, mean_ref, var_ref, pad, read_sem, sem):
    reads = [
        pltpu.make_async_copy(pad_hbm.at[s], pad.at[s], read_sem.at[s]) for s in range(16)
    ]
    writes = [
        pltpu.make_async_copy(
            pad.at[s, half, pl.ds(0, C // 2)], psi_hbm.at[s, :, pl.ds(half * 128, 128)], sem.at[s, half]
        )
        for s in range(16)
        for half in range(2)
    ]
    for copy in reads:
        copy.start()
    for s in range(16):
        reads[s].wait()
        for copy in writes[2 * s : 2 * s + 2]:
            copy.start()
    mean = total[0] / 32.0
    var = total[1] / 32.0 - mean * mean
    shift = (128 - lax.axis_index("lon") * 4) % 128
    mean_ref[...] = pltpu.roll(mean, shift, 1).T[:4, : C // 2]
    var_ref[...] = pltpu.roll(var, shift, 1).T[:4, : C // 2]
    for copy in writes:
        copy.wait()


def overturning(v, h, k, w, width, comm=True):
    dma = pltpu.SemaphoreType.DMA
    hbm = pl.BlockSpec(memory_space=pl.ANY)
    vmem = pl.BlockSpec(memory_space=pltpu.VMEM)
    scratch = [pltpu.VMEM((2, 32, 32, 256), d) for d in (BF16, BF16, jnp.int32, jnp.int32)]
    scratch += [pltpu.VMEM((256, 1024), BF16)] * 8
    scratch += [
        pltpu.VMEM((16, 16, 256), F32),
        pltpu.VMEM((8, 4, 128, 128), F32),
        pltpu.VMEM((8, 3, 128, 128), F32),
        pltpu.VMEM((8, 128, 128), F32),
        pltpu.VMEM((8, 7, 16, 128), F32),
        pltpu.VMEM((8, 16, 128), F32),
        pltpu.VMEM((16, 2, 128, 128), F32),
        pltpu.VMEM((2, 2, 128, 128), F32),
        pltpu.VMEM((2, 128, 128), F32),
        dma((2, 4)), dma((4, 4)), dma((8, 4)),
        dma((9, 3)), dma((9, 3)), dma((9, 7)), dma((9, 7)),
        dma((9, 8)), dma((9, 8)), dma((9, 3)), dma((9, 3)), dma, dma,
    ]
    return pl.pallas_call(
        functools.partial(kernel, comm),
        in_specs=[hbm] * 4 + [vmem],
        out_specs=(hbm, vmem),
        out_shape=(
            jax.ShapeDtypeStruct((16, 2, 128, 128), F32),
            jax.ShapeDtypeStruct((2, 128, 128), F32),
        ),
        scratch_shapes=scratch,
        compiler_params=pltpu.CompilerParams(
            vmem_limit_bytes=56 * 2**20,
            **(dict(collective_id=0, has_side_effects=True) if comm else {}),
        ),
        name="overturning",
    )(v, h, k, w, width)


def shards(velocity, thickness, class_index, layer_weight, zonal_width):
    pad, total = overturning(velocity, thickness, class_index, layer_weight, zonal_width.reshape(2, -1))
    hbm = pl.BlockSpec(memory_space=pl.ANY)
    vmem = pl.BlockSpec(memory_space=pltpu.VMEM)
    psi, mean, var = pl.pallas_call(
        finals,
        in_specs=[hbm, vmem],
        out_specs=(hbm, vmem, vmem),
        out_shape=(
            jax.ShapeDtypeStruct((16, C // 2, 256), F32),
            jax.ShapeDtypeStruct((4, C // 2), F32),
            jax.ShapeDtypeStruct((4, C // 2), F32),
        ),
        scratch_shapes=[
            pltpu.VMEM((16, 2, 128, 128), F32),
            pltpu.SemaphoreType.DMA((16,)),
            pltpu.SemaphoreType.DMA((16, 2)),
        ],
        compiler_params=pltpu.CompilerParams(vmem_limit_bytes=60 * 2**20),
        name="finals",
    )(pad, total)
    return psi, mean.T, var.T


def solution(mesh):
    cells = P("tm", "lon", None, None)
    in_specs = (cells, cells, cells, cells, P())
    out_specs = (P("tm", "cls", None), P("cls", ("tm", "lon")), P("cls", ("tm", "lon")))
    return jax.shard_map(shards, mesh=mesh, in_specs=in_specs, out_specs=out_specs, check_vma=False)
```

```python
import functools
import jax
import jax.numpy as jnp
from jax import lax
from jax.experimental import pallas as pl
from jax.experimental.pallas import tpu as pltpu
from jax.sharding import PartitionSpec as P

C = 240
GROUPS = 8
LAST = 8
NT = (((1,), (1,)), ((), ()))
MESH = pl.DeviceIdType.MESH
F32, BF16 = jnp.float32, jnp.bfloat16


def prepare(raw, turned, chunk):
    lons = pl.ds(chunk * 8, 8)
    cells = pl.ds(pl.multiple_of(chunk * 256, 256), 256)
    for src, dst in zip(raw, turned):
        dst[:, cells] = src[lons].reshape(256, 256).astype(BF16).T


def group_sums(turned, rows):
    total = None
    for start in range(0, 1024, 256):
        cells = slice(start, start + 256)
        v, thick, k, w = (ref[rows, cells] for ref in turned)
        hi = (k.astype(F32) * (1 / 15.0) + (129 - 7 / 15.0)).astype(BF16)
        lo = k - (hi - 129.0) * 15.0
        share = thick.astype(F32) * w.astype(F32)
        q = share.astype(BF16)
        e = (share - q.astype(F32)).astype(BF16)
        h = thick * 64.0
        zero = jnp.zeros_like(v)
        a = jnp.concatenate([jnp.where(hi == float(x + 129), v, zero) for x in range(16)], axis=0)
        b, f = [], []
        below = zero
        for x in range(15):
            here = lo == float(x)
            b.append(jnp.where(here, q, below))
            f.append(jnp.where(here, e, zero))
            below = jnp.where(here, h, below)
        b = jnp.concatenate(b + [below], axis=0)
        f = jnp.concatenate(f + [zero], axis=0)
        part = lax.dot_general(
            jnp.concatenate([b, f], axis=0), a, NT, preferred_element_type=F32
        )
        total = part if total is None else total + part
    total = total[:256] + total[256:]
    return pick(total)


def pick(total):
    lane = lax.broadcasted_iota(jnp.int32, (8, 128), 1)
    sub = lax.broadcasted_iota(jnp.int32, (8, 128), 0)
    blocks = []
    for start in (0, 128):
        cols = slice(start, start + 128)
        upper = (lane & 8) != 0
        x = [
            jnp.where(upper, total[16 * i + 8 : 16 * i + 16, cols], total[16 * i : 16 * i + 8, cols])
            for i in range(16)
        ]
        for d in (4, 2, 1):
            moved = (lane & d) != 0
            stays = (lane & d) == (sub & d)
            y = []
            for i in range(0, len(x), 2 * d):
                for one, two in zip(x[i : i + d], x[i + d : i + 2 * d]):
                    keep = jnp.where(moved, two, one)
                    if d == 4:
                        move = pltpu.roll(jnp.where(moved, one, two), 4, 0)
                    else:
                        move = jnp.where(moved, pltpu.roll(one, 8 - d, 0), pltpu.roll(two, d, 0))
                    y.append(jnp.where(stays, keep, move))
            x = y
        blocks.append(jnp.concatenate(x, axis=0))
    return jnp.concatenate(blocks, axis=1)


def arrange(sums, width, units, slot_of):
    lane = lax.broadcasted_iota(jnp.int32, (16, 128), 1)
    offset = jnp.zeros((1, 128), F32)
    for part in range(2):
        x = [sums[g, :, part * 128 : part * 128 + 128] for g in range(8)]
        for d in (4, 2, 1):
            high = (lane & (16 * d)) != 0
            y = list(x)
            for i in range(8):
                if i & d == 0:
                    if d == 4:
                        move = pltpu.roll(jnp.where(high, x[i], x[i + d]), 64, 1)
                        y[i] = jnp.where(high, move, x[i])
                        y[i + d] = jnp.where(high, x[i + d], move)
                    else:
                        y[i] = jnp.where(high, pltpu.roll(x[i + d], 16 * d, 1), x[i])
                        y[i + d] = jnp.where(high, x[i + d], pltpu.roll(x[i], 128 - 16 * d, 1))
            x = y
        for i in range(8):
            units[slot_of(part), 15 * i : 15 * i + 16, :] = (x[i] + offset) * width
            offset = offset + x[i][15:16]


def kernel(comm, v_hbm, h_hbm, k_hbm, w_hbm, width, psi_hbm, total_ref, *scratch):
    (raw_v, raw_h, raw_k, raw_w), scratch = scratch[:4], scratch[4:]
    even, odd, scratch = scratch[:4], scratch[4:8], scratch[8:]
    (sums, send, got_1, mid, got_2, own, pad, stat, got_3, read_sem, quarter_sem, write_sem) = scratch[:12]
    (s1, r1, s2, r2, s3, r3, s4, r4, s5, r5) = scratch[12:]
    if comm:
        tm, lon, cls = lax.axis_index("tm"), lax.axis_index("lon"), lax.axis_index("cls")
    else:
        tm, lon, cls = jnp.int32(0), jnp.int32(0), jnp.int32(0)
    zz, xx, yy = lon // 8, (lon // 2) % 4, lon % 2
    n_own = 8

    def read(s, slot):
        return [
            pltpu.make_async_copy(src.at[cls * n_own + s], dst.at[slot], read_sem.at[slot, i])
            for i, (src, dst) in enumerate(
                zip((v_hbm, h_hbm, k_hbm, w_hbm), (raw_v, raw_h, raw_k, raw_w))
            )
        ]

    spots = ((xx, zz), (zz, xx))
    cols, col_lon, place, place_lon = [], [], [], []
    for p, (a, b) in enumerate(spots):
        step_a, step_b = (8, 2) if p else (2, 8)
        near = [a] + [(a + rel) % 4 for rel in (1, 2, 3)]
        cols.append(near)
        col_lon.append([c * step_a + b * step_b + yy for c in near])
        me = b * 2 + yy
        near = [me] + [(me + rel) % 8 for rel in range(1, 8)]
        place.append(near)
        place_lon.append([a * step_a + (n // 2) * step_b + n % 2 for n in near])
    home = [(cls + a // 2) % 2 for a, _ in spots]

    def size(job):
        return 128 if job[3] is None else 64

    def unit_of(job, col):
        half = job[3]
        return col, 0 if half is None else half * 64, col % 2

    def base(job, n):
        return 0 if job[3] is None else job[3] * n

    def span(start, n):
        return pl.ds(start if isinstance(start, int) else pl.multiple_of(start, 8), n)

    def first(job, rel):
        i, p, s, _ = job
        n = size(job)
        u, r, _ = unit_of(job, cols[p][rel])
        return pltpu.make_async_remote_copy(
            src_ref=send.at[s, u, span(r, n)], dst_ref=got_1.at[s, 3 - rel, span(base(job, 64), n)],
            send_sem=s1.at[i, rel - 1], recv_sem=r1.at[i, 3 - rel],
            device_id={"lon": col_lon[p][rel]}, device_id_type=MESH)

    def second(job, rel):
        i, p, s, _ = job
        n = size(job) // 8
        return pltpu.make_async_remote_copy(
            src_ref=mid.at[s, span(base(job, 64) + place[p][rel] * n, n)],
            dst_ref=got_2.at[s, 7 - rel, span(base(job, 8), n)],
            send_sem=s2.at[i, rel - 1], recv_sem=r2.at[i, 7 - rel],
            device_id={"lon": place_lon[p][rel]}, device_id_type=MESH)

    def target(job, group, rel):
        _, p, s, _ = job
        n = size(job) // 8
        _, r, half = unit_of(job, cols[p][0])
        return pad.at[group * n_own + s, half, span(r + place[p][rel] * n, n)]

    def third(job, rel):
        i, p, s, _ = job
        return pltpu.make_async_remote_copy(
            src_ref=own.at[s, span(base(job, 8), size(job) // 8)], dst_ref=target(job, cls, 0),
            send_sem=s3.at[i, rel], recv_sem=r3.at[i, (8 - rel) % 8],
            device_id={"lon": place_lon[p][rel], "cls": home[p]}, device_id_type=MESH)

    def third_got(job, rel):
        i, p, s, _ = job
        return pltpu.make_async_remote_copy(
            src_ref=own.at[s, span(base(job, 8), size(job) // 8)], dst_ref=target(job, home[p], rel),
            send_sem=s3.at[i, rel], recv_sem=r3.at[i, rel],
            device_id={"lon": place_lon[p][rel], "cls": home[p]}, device_id_type=MESH)

    def spread(job, rel):
        _, p, s, _ = job
        col = cols[p][rel]
        _, r, half = unit_of(job, col)
        return pad.at[(cls + col // 2) % 2 * n_own + s, half, span(r, size(job))]

    def fourth(job, rel):
        i, p, _, _ = job
        return pltpu.make_async_remote_copy(
            src_ref=spread(job, 0), dst_ref=spread(job, 0), send_sem=s4.at[i, rel - 1],
            recv_sem=r4.at[i, 3 - rel], device_id={"lon": col_lon[p][rel]}, device_id_type=MESH)

    def fourth_got(job, rel):
        i, p, _, _ = job
        dst = spread(job, rel)
        return pltpu.make_async_remote_copy(
            src_ref=dst, dst_ref=dst, send_sem=s4.at[i, rel - 1], recv_sem=r4.at[i, rel - 1],
            device_id={"lon": col_lon[p][rel]}, device_id_type=MESH)

    def write(s):
        return [
            pltpu.make_async_copy(
                pad.at[base + s, half],
                psi_hbm.at[base + s, half],
                write_sem.at[s, base // 4 + half])
            for base in (0, n_own) for half in (0, 1)
        ]

    def start_1(job):
        for rel in (1, 2, 3):
            first(job, rel).start()

    def start_2(job):
        _, p, s, _ = job
        n = size(job)
        u, r, _ = unit_of(job, cols[p][0])
        rows = span(base(job, 64), n)
        for rel in (1, 2, 3):
            first(job, rel).wait_recv()
        mid[s, rows] = send[s, u, span(r, n)] + got_1[s, 0, rows] + got_1[s, 1, rows] + got_1[s, 2, rows]
        for rel in range(1, 8):
            second(job, rel).start()

    def start_3(job):
        _, p, s, _ = job
        n = size(job) // 8
        rows = span(base(job, 8), n)
        for rel in range(1, 8):
            second(job, rel).wait_recv()
        total = mid[s, span(base(job, 64) + place[p][0] * n, n)]
        for i in range(7):
            total = total + got_2[s, i, rows]
        own[s, rows] = total

        @pl.when(cols[p][0] < 2)
        def _():
            target(job, cls, 0)[...] = total

        @pl.when(cols[p][0] >= 2)
        def _():
            third(job, 0).start()

        for rel in range(1, 8):
            third(job, rel).start()

    def start_4(job):
        p = job[1]

        @pl.when(cols[p][0] >= 2)
        def _():
            third_got(job, 0).wait_recv()

        for rel in range(1, 8):
            third_got(job, rel).wait_recv()
        for rel in (1, 2, 3):
            fourth(job, rel).start()

    def take(s):
        for half in range(2):
            one, two = stat[half, 0], stat[half, 1]
            for base in (0, n_own):
                x = pad[base + s, half]
                one = one + x
                two = two + x * x
            stat[half, 0] = one
            stat[half, 1] = two

    def finish(job):
        for rel in (1, 2, 3):
            fourth_got(job, rel).wait_recv()
        if job[0] is not LAST - 1:
            for copy in write(job[2]):
                copy.start()
            take(job[2])

    def drain(job):
        for rel in (1, 2, 3):
            first(job, rel).wait_send()
            fourth(job, rel).wait_send()
        for rel in range(1, 8):
            second(job, rel).wait_send()
            third(job, rel).wait_send()

        @pl.when(cols[job[1]][0] >= 2)
        def _():
            third(job, 0).wait_send()

        if job[0] is not LAST - 1:
            for copy in write(job[2]):
                copy.wait()

    def whole(q, s):
        return (s, q, s, None)

    ends = ((LAST - 1, 1, 7, 0), (LAST, 0, 7, 1))

    barrier = None
    if comm:
        barrier = pltpu.get_barrier_semaphore()
        def greet(to, where):
            pl.semaphore_signal(barrier, inc=1, device_id=where, device_id_type=MESH)

        for y in range(2):
            for i in range(4):
                for near in range(2):
                    group = (cls + near) % 2
                    row = {"lon": ((zz + i) % 4) * 8 + xx * 2 + (yy + y) % 2, "cls": group}
                    if near or i or y:
                        greet(None, row)
                    if i:
                        greet(None, {"lon": zz * 8 + ((xx + i) % 4) * 2 + (yy + y) % 2, "cls": group})
        greet(None, {"tm": 1 - tm})
    n_greet = 2 * 2 * 4 - 1 + 2 * 2 * 3 + 1

    raws = [[ref.at[slot] for ref in (raw_v, raw_h, raw_k, raw_w)] for slot in range(2)]

    def quarter(chunk):
        lons = pl.ds(chunk * 8, 8)
        return [
            pltpu.make_async_copy(src.at[cls * n_own, lons], dst.at[0, lons], quarter_sem.at[chunk, i])
            for i, (src, dst) in enumerate(
                zip((v_hbm, h_hbm, k_hbm, w_hbm), (raw_v, raw_h, raw_k, raw_w))
            )
        ]

    for chunk in range(4):
        for copy in quarter(chunk):
            copy.start()
    for copy in read(1, 1):
        copy.start()
    stat[...] = jnp.zeros_like(stat)
    def pad_rows(s, carry):
        for u in range(4):
            send[s, u, pl.ds(C // 2, 8), :] = jnp.zeros((8, 128), F32)
        return carry

    lax.fori_loop(0, n_own, pad_rows, 0)

    def prologue(chunk, carry):
        for copy in quarter(chunk):
            copy.wait()
        prepare(raws[0], even, chunk)
        return carry

    lax.fori_loop(0, 4, prologue, 0)

    def compute(s, p):
        here, there = (odd, even) if p else (even, odd)

        @pl.when(s + 2 < n_own)
        def _():
            for copy in read(s + 2, p):
                copy.start()

        @pl.when(s + 1 < n_own)
        def _():
            for copy in read(s + 1, 1 - p):
                copy.wait()

        def run(more):
            def step(j, carry):
                for c in range(GROUPS // 4 if more else 0):
                    prepare(raws[1 - p], there, j * (GROUPS // 4) + c)
                for g in range(GROUPS):
                    rows = pl.ds(pl.multiple_of((j * GROUPS + g) * 16, 16), 16)
                    sums[j * GROUPS + g] = group_sums(here, rows)
                return carry

            lax.fori_loop(0, 16 // GROUPS, step, 0)

        if p == 0:
            run(True)
        else:
            pl.when(s < n_own - 1)(lambda: run(True))
            pl.when(s == n_own - 1)(lambda: run(False))
        for j in range(2):
            arrange(sums.at[pl.ds(j * 8, 8)], width[j : j + 1, :] * (1 / 64.0), send.at[s], lambda cut: ((cls + cut) % 2) * 2 + j)

    def pair(t, carry):
        for p in range(2):
            s = 2 * t + p
            compute(s, p)
            if not comm:
                continue

            def advance():
                start_1(whole(p, s))
                for least, go, q in ((1, start_2, 1 - p), (2, start_3, p), (3, start_4, 1 - p), (4, finish, p)):
                    if least <= p:
                        go(whole(q, s - least))
                    else:
                        @pl.when(s >= least)
                        def _(go=go, q=q, least=least):
                            go(whole(q, s - least))

            if p == 0:
                @pl.when(t == 0)
                def _():
                    pl.semaphore_wait(barrier, n_greet)
                advance()
            else:
                pl.when(s < n_own - 1)(advance)
        return carry

    lax.fori_loop(0, n_own // 2, pair, 0)
    if comm:
        for job in ends:
            start_1(job)
        start_2(whole(0, 6))
        start_3(whole(1, 5))
        start_4(whole(0, 4))
        finish(whole(1, 3))
        for job in ends:
            start_2(job)
        start_3(whole(0, 6))
        start_4(whole(1, 5))
        finish(whole(0, 4))
        for job in ends:
            start_3(job)
        start_4(whole(0, 6))
        finish(whole(1, 5))
        for job in ends:
            start_4(job)
        finish(whole(0, 6))
        for job in ends:
            finish(job)
        swap = pltpu.make_async_remote_copy(
            src_ref=stat.at[1 - tm], dst_ref=got_3, send_sem=s5, recv_sem=r5,
            device_id={"tm": 1 - tm}, device_id_type=MESH)
        swap.start()

        def drains(t, carry):
            drain(whole(0, 2 * t))
            drain(whole(1, 2 * t + 1))
            return carry

        lax.fori_loop(0, n_own // 2 - 1, drains, 0)
        drain(whole(0, 6))
        for job in ends:
            drain(job)
        swap.wait()
    else:
        for s in range(8):
            pad[s, 0] = send[s, 0]
            pad[s, 1] = send[s, 1]
            pad[s + 8, 0] = send[s, 2]
            pad[s + 8, 1] = send[s, 3]
        for s in (0, 7):
            for copy in write(s):
                copy.start()
            for copy in write(s):
                copy.wait()
        got_3[...] = jnp.zeros_like(got_3)
    total_ref[...] = stat[tm] + got_3[...]


def finals(pad_hbm, total_hbm, psi_hbm, mean_hbm, var_hbm, pad, total, mean_ref, var_ref, read_sem, sem, stat_sem):
    reads = [
        pltpu.make_async_copy(pad_hbm.at[s], pad.at[s], read_sem.at[s]) for s in range(16)
    ]
    writes = [
        pltpu.make_async_copy(
            pad.at[s, half, pl.ds(0, C // 2)], psi_hbm.at[s, :, pl.ds(half * 128, 128)], sem.at[s, half]
        )
        for s in range(16)
        for half in range(2)
    ]
    sums = pltpu.make_async_copy(total_hbm, total, stat_sem.at[0])
    stats = [
        pltpu.make_async_copy(mean_ref, mean_hbm, stat_sem.at[1]),
        pltpu.make_async_copy(var_ref, var_hbm, stat_sem.at[2]),
    ]
    sums.start()
    for copy in reads:
        copy.start()
    sums.wait()
    mean = total[0] / 32.0
    var = total[1] / 32.0 - mean * mean
    shift = (128 - lax.axis_index("lon") * 4) % 128
    mean_ref[...] = pltpu.roll(mean, shift, 1).T[:4, : C // 2]
    var_ref[...] = pltpu.roll(var, shift, 1).T[:4, : C // 2]
    for copy in stats:
        copy.start()
    for s in range(16):
        reads[s].wait()
        for copy in writes[2 * s : 2 * s + 2]:
            copy.start()
    for copy in writes + stats:
        copy.wait()


def overturning(v, h, k, w, width, comm=True):
    dma = pltpu.SemaphoreType.DMA
    hbm = pl.BlockSpec(memory_space=pl.ANY)
    vmem = pl.BlockSpec(memory_space=pltpu.VMEM)
    scratch = [pltpu.VMEM((2, 32, 32, 256), d) for d in (BF16, BF16, jnp.int32, jnp.int32)]
    scratch += [pltpu.VMEM((256, 1024), BF16)] * 8
    scratch += [
        pltpu.VMEM((16, 16, 256), F32),
        pltpu.VMEM((8, 4, 128, 128), F32),
        pltpu.VMEM((8, 3, 128, 128), F32),
        pltpu.VMEM((8, 128, 128), F32),
        pltpu.VMEM((8, 7, 16, 128), F32),
        pltpu.VMEM((8, 16, 128), F32),
        pltpu.VMEM((16, 2, 128, 128), F32),
        pltpu.VMEM((2, 2, 128, 128), F32),
        pltpu.VMEM((2, 128, 128), F32),
        dma((2, 4)), dma((4, 4)), dma((8, 4)),
        dma((9, 3)), dma((9, 3)), dma((9, 7)), dma((9, 7)),
        dma((9, 8)), dma((9, 8)), dma((9, 3)), dma((9, 3)), dma, dma,
    ]
    return pl.pallas_call(
        functools.partial(kernel, comm),
        in_specs=[hbm] * 4 + [vmem],
        out_specs=(hbm, vmem),
        out_shape=(
            jax.ShapeDtypeStruct((16, 2, 128, 128), F32),
            jax.ShapeDtypeStruct((2, 128, 128), F32),
        ),
        scratch_shapes=scratch,
        compiler_params=pltpu.CompilerParams(
            vmem_limit_bytes=56 * 2**20,
            **(dict(collective_id=0, has_side_effects=True) if comm else {}),
        ),
        name="overturning",
    )(v, h, k, w, width)


def shards(velocity, thickness, class_index, layer_weight, zonal_width):
    pad, total = overturning(velocity, thickness, class_index, layer_weight, zonal_width.reshape(2, -1))
    hbm = pl.BlockSpec(memory_space=pl.ANY)
    vmem = pl.BlockSpec(memory_space=pltpu.VMEM)
    psi, mean, var = pl.pallas_call(
        finals,
        in_specs=[hbm, hbm],
        out_specs=(hbm, hbm, hbm),
        out_shape=(
            jax.ShapeDtypeStruct((16, C // 2, 256), F32),
            jax.ShapeDtypeStruct((4, C // 2), F32),
            jax.ShapeDtypeStruct((4, C // 2), F32),
        ),
        scratch_shapes=[
            pltpu.VMEM((16, 2, 128, 128), F32),
            pltpu.VMEM((2, 128, 128), F32),
            pltpu.VMEM((4, C // 2), F32),
            pltpu.VMEM((4, C // 2), F32),
            pltpu.SemaphoreType.DMA((16,)),
            pltpu.SemaphoreType.DMA((16, 2)),
            pltpu.SemaphoreType.DMA((3,)),
        ],
        compiler_params=pltpu.CompilerParams(vmem_limit_bytes=60 * 2**20),
        name="finals",
    )(pad, total)
    return psi, mean.T, var.T


def solution(mesh):
    cells = P("tm", "lon", None, None)
    in_specs = (cells, cells, cells, cells, P())
    out_specs = (P("tm", "cls", None), P("cls", ("tm", "lon")), P("cls", ("tm", "lon")))
    return jax.shard_map(shards, mesh=mesh, in_specs=in_specs, out_specs=out_specs, check_vma=False)
```

```python
import functools
import jax
import jax.numpy as jnp
from jax import lax
from jax.experimental import pallas as pl
from jax.experimental.pallas import tpu as pltpu
from jax.sharding import PartitionSpec as P

C = 240
GROUPS = 8
LAST = 8
NT = (((1,), (1,)), ((), ()))
MESH = pl.DeviceIdType.MESH
F32, BF16 = jnp.float32, jnp.bfloat16


def prepare(raw, turned, chunk):
    lons = pl.ds(chunk * 8, 8)
    cells = pl.ds(pl.multiple_of(chunk * 256, 256), 256)
    for src, dst in zip(raw, turned):
        dst[:, cells] = src[lons].reshape(256, 256).astype(BF16).T


def group_sums(turned, rows):
    total = None
    for start in range(0, 1024, 256):
        cells = slice(start, start + 256)
        v, thick, k, w = (ref[rows, cells] for ref in turned)
        hi = (k.astype(F32) * (1 / 15.0) + (129 - 7 / 15.0)).astype(BF16)
        lo = k - (hi - 129.0) * 15.0
        share = thick.astype(F32) * w.astype(F32)
        q = share.astype(BF16)
        e = (share - q.astype(F32)).astype(BF16)
        h = thick * 64.0
        zero = jnp.zeros_like(v)
        a = jnp.concatenate([jnp.where(hi == float(x + 129), v, zero) for x in range(16)], axis=0)
        b, f = [], []
        below = zero
        for x in range(15):
            here = lo == float(x)
            b.append(jnp.where(here, q, below))
            f.append(jnp.where(here, e, zero))
            below = jnp.where(here, h, below)
        b = jnp.concatenate(b + [below], axis=0)
        f = jnp.concatenate(f + [zero], axis=0)
        part = lax.dot_general(
            jnp.concatenate([b, f], axis=0), a, NT, preferred_element_type=F32
        )
        total = part if total is None else total + part
    total = total[:256] + total[256:]
    return pick(total)


def pick(total):
    lane = lax.broadcasted_iota(jnp.int32, (8, 128), 1)
    sub = lax.broadcasted_iota(jnp.int32, (8, 128), 0)
    blocks = []
    for start in (0, 128):
        cols = slice(start, start + 128)
        upper = (lane & 8) != 0
        x = [
            jnp.where(upper, total[16 * i + 8 : 16 * i + 16, cols], total[16 * i : 16 * i + 8, cols])
            for i in range(16)
        ]
        for d in (4, 2, 1):
            moved = (lane & d) != 0
            stays = (lane & d) == (sub & d)
            y = []
            for i in range(0, len(x), 2 * d):
                for one, two in zip(x[i : i + d], x[i + d : i + 2 * d]):
                    keep = jnp.where(moved, two, one)
                    if d == 4:
                        move = pltpu.roll(jnp.where(moved, one, two), 4, 0)
                    else:
                        move = jnp.where(moved, pltpu.roll(one, 8 - d, 0), pltpu.roll(two, d, 0))
                    y.append(jnp.where(stays, keep, move))
            x = y
        blocks.append(jnp.concatenate(x, axis=0))
    return jnp.concatenate(blocks, axis=1)


def arrange(sums, width, units, slot_of):
    lane = lax.broadcasted_iota(jnp.int32, (16, 128), 1)
    offset = jnp.zeros((1, 128), F32)
    for part in range(2):
        x = [sums[g, :, part * 128 : part * 128 + 128] for g in range(8)]
        for d in (4, 2, 1):
            high = (lane & (16 * d)) != 0
            y = list(x)
            for i in range(8):
                if i & d == 0:
                    if d == 4:
                        move = pltpu.roll(jnp.where(high, x[i], x[i + d]), 64, 1)
                        y[i] = jnp.where(high, move, x[i])
                        y[i + d] = jnp.where(high, x[i + d], move)
                    else:
                        y[i] = jnp.where(high, pltpu.roll(x[i + d], 16 * d, 1), x[i])
                        y[i + d] = jnp.where(high, x[i + d], pltpu.roll(x[i], 128 - 16 * d, 1))
            x = y
        for i in range(8):
            units[slot_of(part), 15 * i : 15 * i + 16, :] = (x[i] + offset) * width
            offset = offset + x[i][15:16]


def kernel(comm, v_hbm, h_hbm, k_hbm, w_hbm, width, psi_hbm, total_ref, *scratch):
    (raw_v, raw_h, raw_k, raw_w), scratch = scratch[:4], scratch[4:]
    even, odd, scratch = scratch[:4], scratch[4:8], scratch[8:]
    (sums, send, got_1, mid, got_2, own, pad, stat, got_3, read_sem, quarter_sem, write_sem) = scratch[:12]
    (s1, r1, s2, r2, s3, r3, s4, r4, s5, r5) = scratch[12:]
    if comm:
        tm, lon, cls = lax.axis_index("tm"), lax.axis_index("lon"), lax.axis_index("cls")
    else:
        tm, lon, cls = jnp.int32(0), jnp.int32(0), jnp.int32(0)
    zz, xx, yy = lon // 8, (lon // 2) % 4, lon % 2
    n_own = 8

    def read(s, slot):
        return [
            pltpu.make_async_copy(src.at[cls * n_own + s], dst.at[slot], read_sem.at[slot, i])
            for i, (src, dst) in enumerate(
                zip((v_hbm, h_hbm, k_hbm, w_hbm), (raw_v, raw_h, raw_k, raw_w))
            )
        ]

    spots = ((xx, zz), (zz, xx))
    cols, col_lon, place, place_lon = [], [], [], []
    for p, (a, b) in enumerate(spots):
        step_a, step_b = (8, 2) if p else (2, 8)
        near = [a] + [(a + rel) % 4 for rel in (1, 2, 3)]
        cols.append(near)
        col_lon.append([c * step_a + b * step_b + yy for c in near])
        me = b * 2 + yy
        near = [me] + [(me + rel) % 8 for rel in range(1, 8)]
        place.append(near)
        place_lon.append([a * step_a + (n // 2) * step_b + n % 2 for n in near])
    home = [(cls + a // 2) % 2 for a, _ in spots]

    def size(job):
        return 128 if job[3] is None else 64

    def unit_of(job, col):
        half = job[3]
        return col, 0 if half is None else half * 64, col % 2

    def base(job, n):
        return 0 if job[3] is None else job[3] * n

    def span(start, n):
        return pl.ds(start if isinstance(start, int) else pl.multiple_of(start, 8), n)

    def first(job, rel):
        i, p, s, _ = job
        n = size(job)
        u, r, _ = unit_of(job, cols[p][rel])
        return pltpu.make_async_remote_copy(
            src_ref=send.at[s, u, span(r, n)], dst_ref=got_1.at[s, 3 - rel, span(base(job, 64), n)],
            send_sem=s1.at[i, rel - 1], recv_sem=r1.at[i, 3 - rel],
            device_id={"lon": col_lon[p][rel]}, device_id_type=MESH)

    def second(job, rel):
        i, p, s, _ = job
        n = size(job) // 8
        return pltpu.make_async_remote_copy(
            src_ref=mid.at[s, span(base(job, 64) + place[p][rel] * n, n)],
            dst_ref=got_2.at[s, 7 - rel, span(base(job, 8), n)],
            send_sem=s2.at[i, rel - 1], recv_sem=r2.at[i, 7 - rel],
            device_id={"lon": place_lon[p][rel]}, device_id_type=MESH)

    def target(job, group, rel):
        _, p, s, _ = job
        n = size(job) // 8
        _, r, half = unit_of(job, cols[p][0])
        return pad.at[group * n_own + s, half, span(r + place[p][rel] * n, n)]

    def third(job, rel):
        i, p, s, _ = job
        return pltpu.make_async_remote_copy(
            src_ref=own.at[s, span(base(job, 8), size(job) // 8)], dst_ref=target(job, cls, 0),
            send_sem=s3.at[i, rel], recv_sem=r3.at[i, (8 - rel) % 8],
            device_id={"lon": place_lon[p][rel], "cls": home[p]}, device_id_type=MESH)

    def third_got(job, rel):
        i, p, s, _ = job
        return pltpu.make_async_remote_copy(
            src_ref=own.at[s, span(base(job, 8), size(job) // 8)], dst_ref=target(job, home[p], rel),
            send_sem=s3.at[i, rel], recv_sem=r3.at[i, rel],
            device_id={"lon": place_lon[p][rel], "cls": home[p]}, device_id_type=MESH)

    def spread(job, rel):
        _, p, s, _ = job
        col = cols[p][rel]
        _, r, half = unit_of(job, col)
        return pad.at[(cls + col // 2) % 2 * n_own + s, half, span(r, size(job))]

    def fourth(job, rel):
        i, p, _, _ = job
        return pltpu.make_async_remote_copy(
            src_ref=spread(job, 0), dst_ref=spread(job, 0), send_sem=s4.at[i, rel - 1],
            recv_sem=r4.at[i, 3 - rel], device_id={"lon": col_lon[p][rel]}, device_id_type=MESH)

    def fourth_got(job, rel):
        i, p, _, _ = job
        dst = spread(job, rel)
        return pltpu.make_async_remote_copy(
            src_ref=dst, dst_ref=dst, send_sem=s4.at[i, rel - 1], recv_sem=r4.at[i, rel - 1],
            device_id={"lon": col_lon[p][rel]}, device_id_type=MESH)

    def write(s):
        return [
            pltpu.make_async_copy(
                pad.at[base + s, half],
                psi_hbm.at[base + s, half],
                write_sem.at[s, base // 4 + half])
            for base in (0, n_own) for half in (0, 1)
        ]

    def start_1(job):
        for rel in (1, 2, 3):
            first(job, rel).start()

    def start_2(job):
        _, p, s, _ = job
        n = size(job)
        u, r, _ = unit_of(job, cols[p][0])
        rows = span(base(job, 64), n)
        for rel in (1, 2, 3):
            first(job, rel).wait_recv()
        mid[s, rows] = send[s, u, span(r, n)] + got_1[s, 0, rows] + got_1[s, 1, rows] + got_1[s, 2, rows]
        for rel in range(1, 8):
            second(job, rel).start()

    def start_3(job):
        _, p, s, _ = job
        n = size(job) // 8
        rows = span(base(job, 8), n)
        for rel in range(1, 8):
            second(job, rel).wait_recv()
        total = mid[s, span(base(job, 64) + place[p][0] * n, n)]
        for i in range(7):
            total = total + got_2[s, i, rows]
        own[s, rows] = total

        @pl.when(cols[p][0] < 2)
        def _():
            target(job, cls, 0)[...] = total

        @pl.when(cols[p][0] >= 2)
        def _():
            third(job, 0).start()

        for rel in range(1, 8):
            third(job, rel).start()

    def start_4(job):
        p = job[1]

        @pl.when(cols[p][0] >= 2)
        def _():
            third_got(job, 0).wait_recv()

        for rel in range(1, 8):
            third_got(job, rel).wait_recv()
        for rel in (1, 2, 3):
            fourth(job, rel).start()

    def take(s):
        for half in range(2):
            one, two = stat[half, 0], stat[half, 1]
            for base in (0, n_own):
                x = pad[base + s, half]
                one = one + x
                two = two + x * x
            stat[half, 0] = one
            stat[half, 1] = two

    def finish(job):
        for rel in (1, 2, 3):
            fourth_got(job, rel).wait_recv()
        if job[0] is not LAST - 1:
            for copy in write(job[2]):
                copy.start()
            take(job[2])

    def drain(job):
        for rel in (1, 2, 3):
            first(job, rel).wait_send()
            fourth(job, rel).wait_send()
        for rel in range(1, 8):
            second(job, rel).wait_send()
            third(job, rel).wait_send()

        @pl.when(cols[job[1]][0] >= 2)
        def _():
            third(job, 0).wait_send()

        if job[0] is not LAST - 1:
            for copy in write(job[2]):
                copy.wait()

    def whole(q, s):
        return (s, q, s, None)

    ends = ((LAST - 1, 1, 7, 0), (LAST, 0, 7, 1))

    barrier = None
    if comm:
        barrier = pltpu.get_barrier_semaphore()
        def greet(to, where):
            pl.semaphore_signal(barrier, inc=1, device_id=where, device_id_type=MESH)

        for y in range(2):
            for i in range(4):
                for near in range(2):
                    group = (cls + near) % 2
                    row = {"lon": ((zz + i) % 4) * 8 + xx * 2 + (yy + y) % 2, "cls": group}
                    if near or i or y:
                        greet(None, row)
                    if i:
                        greet(None, {"lon": zz * 8 + ((xx + i) % 4) * 2 + (yy + y) % 2, "cls": group})
        greet(None, {"tm": 1 - tm})
    n_greet = 2 * 2 * 4 - 1 + 2 * 2 * 3 + 1

    raws = [[ref.at[slot] for ref in (raw_v, raw_h, raw_k, raw_w)] for slot in range(2)]

    def quarter(chunk):
        lons = pl.ds(chunk * 8, 8)
        return [
            pltpu.make_async_copy(src.at[cls * n_own, lons], dst.at[0, lons], quarter_sem.at[chunk, i])
            for i, (src, dst) in enumerate(
                zip((v_hbm, h_hbm, k_hbm, w_hbm), (raw_v, raw_h, raw_k, raw_w))
            )
        ]

    for chunk in range(4):
        for copy in quarter(chunk):
            copy.start()
    for copy in read(1, 1):
        copy.start()
    stat[...] = jnp.zeros_like(stat)
    def pad_rows(s, carry):
        for u in range(4):
            send[s, u, pl.ds(C // 2, 8), :] = jnp.zeros((8, 128), F32)
        return carry

    lax.fori_loop(0, n_own, pad_rows, 0)

    def prologue(chunk, carry):
        for copy in quarter(chunk):
            copy.wait()
        prepare(raws[0], even, chunk)
        return carry

    lax.fori_loop(0, 4, prologue, 0)

    def compute(s, p):
        here, there = (odd, even) if p else (even, odd)

        @pl.when(s + 2 < n_own)
        def _():
            for copy in read(s + 2, p):
                copy.start()

        @pl.when(s + 1 < n_own)
        def _():
            for copy in read(s + 1, 1 - p):
                copy.wait()

        def lay_out(j):
            arrange(
                sums.at[pl.ds(j * 8, 8)], width[pl.ds(j, 1), :] * (1 / 64.0), send.at[s],
                lambda cut: ((cls + cut) % 2) * 2 + j)

        def run(more):
            def step(j, carry):
                for c in range(GROUPS // 4 if more else 0):
                    prepare(raws[1 - p], there, j * (GROUPS // 4) + c)
                for g in range(GROUPS):
                    rows = pl.ds(pl.multiple_of((j * GROUPS + g) * 16, 16), 16)
                    sums[j * GROUPS + g] = group_sums(here, rows)
                if not more:
                    lay_out(j)
                    for job in ends:
                        for rel in (1, 2, 3):
                            @pl.when(cols[job[1]][rel] % 2 == j)
                            def _(job=job, rel=rel):
                                first(job, rel).start()
                return carry

            lax.fori_loop(0, 16 // GROUPS, step, 0)

        if p == 0:
            run(True)
        else:
            pl.when(s < n_own - 1)(lambda: run(True))
            pl.when(s == n_own - 1)(lambda: run(False))
        def both():
            for j in range(2):
                lay_out(j)

        if p == 0:
            both()
        else:
            pl.when(s < n_own - 1)(both)

    def pair(t, carry):
        for p in range(2):
            s = 2 * t + p
            compute(s, p)
            if not comm:
                continue

            def advance():
                start_1(whole(p, s))
                for least, go, q in ((1, start_2, 1 - p), (2, start_3, p), (3, start_4, 1 - p), (4, finish, p)):
                    if least <= p:
                        go(whole(q, s - least))
                    else:
                        @pl.when(s >= least)
                        def _(go=go, q=q, least=least):
                            go(whole(q, s - least))

            if p == 0:
                @pl.when(t == 0)
                def _():
                    pl.semaphore_wait(barrier, n_greet)
                advance()
            else:
                pl.when(s < n_own - 1)(advance)
        return carry

    lax.fori_loop(0, n_own // 2, pair, 0)
    if comm:
        start_2(whole(0, 6))
        start_3(whole(1, 5))
        start_4(whole(0, 4))
        finish(whole(1, 3))
        for job in ends:
            start_2(job)
        start_3(whole(0, 6))
        start_4(whole(1, 5))
        finish(whole(0, 4))
        for job in ends:
            start_3(job)
        start_4(whole(0, 6))
        finish(whole(1, 5))
        for job in ends:
            start_4(job)
        finish(whole(0, 6))
        for job in ends:
            finish(job)
        swap = pltpu.make_async_remote_copy(
            src_ref=stat.at[1 - tm], dst_ref=got_3, send_sem=s5, recv_sem=r5,
            device_id={"tm": 1 - tm}, device_id_type=MESH)
        swap.start()

        def drains(t, carry):
            drain(whole(0, 2 * t))
            drain(whole(1, 2 * t + 1))
            return carry

        lax.fori_loop(0, n_own // 2 - 1, drains, 0)
        drain(whole(0, 6))
        for job in ends:
            drain(job)
        swap.wait()
    else:
        for s in range(8):
            pad[s, 0] = send[s, 0]
            pad[s, 1] = send[s, 1]
            pad[s + 8, 0] = send[s, 2]
            pad[s + 8, 1] = send[s, 3]
        for s in (0, 7):
            for copy in write(s):
                copy.start()
            for copy in write(s):
                copy.wait()
        got_3[...] = jnp.zeros_like(got_3)
    total_ref[...] = stat[tm] + got_3[...]


def finals(pad_hbm, total_hbm, psi_hbm, mean_hbm, var_hbm, pad, total, mean_ref, var_ref, read_sem, sem, stat_sem):
    reads = [
        pltpu.make_async_copy(pad_hbm.at[s], pad.at[s], read_sem.at[s]) for s in range(16)
    ]
    writes = [
        pltpu.make_async_copy(
            pad.at[s, half, pl.ds(0, C // 2)], psi_hbm.at[s, :, pl.ds(half * 128, 128)], sem.at[s, half]
        )
        for s in range(16)
        for half in range(2)
    ]
    sums = pltpu.make_async_copy(total_hbm, total, stat_sem.at[0])
    stats = [
        pltpu.make_async_copy(mean_ref, mean_hbm, stat_sem.at[1]),
        pltpu.make_async_copy(var_ref, var_hbm, stat_sem.at[2]),
    ]
    sums.start()
    for copy in reads:
        copy.start()
    sums.wait()
    mean = total[0] / 32.0
    var = total[1] / 32.0 - mean * mean
    shift = (128 - lax.axis_index("lon") * 4) % 128
    mean_ref[...] = pltpu.roll(mean, shift, 1).T[:4, : C // 2]
    var_ref[...] = pltpu.roll(var, shift, 1).T[:4, : C // 2]
    for copy in stats:
        copy.start()
    for s in range(16):
        reads[s].wait()
        for copy in writes[2 * s : 2 * s + 2]:
            copy.start()
    for copy in writes + stats:
        copy.wait()


def overturning(v, h, k, w, width, comm=True):
    dma = pltpu.SemaphoreType.DMA
    hbm = pl.BlockSpec(memory_space=pl.ANY)
    vmem = pl.BlockSpec(memory_space=pltpu.VMEM)
    scratch = [pltpu.VMEM((2, 32, 32, 256), d) for d in (BF16, BF16, jnp.int32, jnp.int32)]
    scratch += [pltpu.VMEM((256, 1024), BF16)] * 8
    scratch += [
        pltpu.VMEM((16, 16, 256), F32),
        pltpu.VMEM((8, 4, 128, 128), F32),
        pltpu.VMEM((8, 3, 128, 128), F32),
        pltpu.VMEM((8, 128, 128), F32),
        pltpu.VMEM((8, 7, 16, 128), F32),
        pltpu.VMEM((8, 16, 128), F32),
        pltpu.VMEM((16, 2, 128, 128), F32),
        pltpu.VMEM((2, 2, 128, 128), F32),
        pltpu.VMEM((2, 128, 128), F32),
        dma((2, 4)), dma((4, 4)), dma((8, 4)),
        dma((9, 3)), dma((9, 3)), dma((9, 7)), dma((9, 7)),
        dma((9, 8)), dma((9, 8)), dma((9, 3)), dma((9, 3)), dma, dma,
    ]
    return pl.pallas_call(
        functools.partial(kernel, comm),
        in_specs=[hbm] * 4 + [vmem],
        out_specs=(hbm, vmem),
        out_shape=(
            jax.ShapeDtypeStruct((16, 2, 128, 128), F32),
            jax.ShapeDtypeStruct((2, 128, 128), F32),
        ),
        scratch_shapes=scratch,
        compiler_params=pltpu.CompilerParams(
            vmem_limit_bytes=56 * 2**20,
            **(dict(collective_id=0, has_side_effects=True) if comm else {}),
        ),
        name="overturning",
    )(v, h, k, w, width)


def shards(velocity, thickness, class_index, layer_weight, zonal_width):
    pad, total = overturning(velocity, thickness, class_index, layer_weight, zonal_width.reshape(2, -1))
    hbm = pl.BlockSpec(memory_space=pl.ANY)
    vmem = pl.BlockSpec(memory_space=pltpu.VMEM)
    psi, mean, var = pl.pallas_call(
        finals,
        in_specs=[hbm, hbm],
        out_specs=(hbm, hbm, hbm),
        out_shape=(
            jax.ShapeDtypeStruct((16, C // 2, 256), F32),
            jax.ShapeDtypeStruct((4, C // 2), F32),
            jax.ShapeDtypeStruct((4, C // 2), F32),
        ),
        scratch_shapes=[
            pltpu.VMEM((16, 2, 128, 128), F32),
            pltpu.VMEM((2, 128, 128), F32),
            pltpu.VMEM((4, C // 2), F32),
            pltpu.VMEM((4, C // 2), F32),
            pltpu.SemaphoreType.DMA((16,)),
            pltpu.SemaphoreType.DMA((16, 2)),
            pltpu.SemaphoreType.DMA((3,)),
        ],
        compiler_params=pltpu.CompilerParams(vmem_limit_bytes=60 * 2**20),
        name="finals",
    )(pad, total)
    return psi, mean.T, var.T


def solution(mesh):
    cells = P("tm", "lon", None, None)
    in_specs = (cells, cells, cells, cells, P())
    out_specs = (P("tm", "cls", None), P("cls", ("tm", "lon")), P("cls", ("tm", "lon")))
    return jax.shard_map(shards, mesh=mesh, in_specs=in_specs, out_specs=out_specs, check_vma=False)
```
